32 devices in a mesh: die: 2 (over y), row: 4 (over z), col: 4 (over x, core).
Axes of the slice: x: 2, y: 2, z: 4, core: 2. Of those that a mesh axis runs over, the one named last changes fastest.
Arguments:
- parcel_patch: float32 [4, 2048, 256], P('die', ('row', 'col')), may hold values from 0.1 to 1
- target_unit: int32 [4, 2048, 1], P('die', ('row', 'col')), may hold values from 0 to 15; in each aligned block of 128 rows (0 to 127, 128 to 255, ..., all dimensions but the last counted through in order) at most 16 rows name the same one
- target_patch: int32 [4, 2048], P('die', ('row', 'col')), may hold values from 0 to 127
- across_taps: float32 [8, 255], replicated, may hold values from -0.375 to 0.375
- down_taps: float32 [8, 255], replicated, may hold values from -0.375 to 0.375
- source_heated_mixing: float32 [8, 4, 4], replicated, may hold values from -2.4 to 2.4
Outputs:
- chip_heat_increase: float32 [4, 512, 1024], P('die', 'row', 'col')
- block_power_slopes: float32 [4, 2048, 256], P('die', ('row', 'col'))
The draws below stay inside these ranges and needn't reach their ends.
Inputs may be any that keep to these rules, and one draw needn't show every extreme that they name: `target_unit`: among the 128 blocks of one die held by one device (aligned blocks of rows), at most 16 name the same device, and in every draw some such group names one device exactly 16 times.
All inputs are finite; a program needn't handle non-finite values.
Results may differ from the reference program's by a relative error of at most 0.0002.
Values sent between devices are 32-bit elements; how exact they have to be, the bound alone decides.
A program may use at most 192 MiB of HBM per device.

```python
import math
import jax
import jax.numpy as jnp
import numpy as np
from jax import lax

STACK_CHIPS = 4
KERNEL_MODES = 8
TAPS = 255
PATCH_SIDE = 16
UNIT_MESH_X = 128
UNIT_MESH_Y = 256
PARCELS_PER_UNIT = 128
PARCELS = 2048
PARCEL_LIMIT = 16
PATCH_AREA = 256
CELLS_ALONG_ONE = 512
CELLS_ALONG_TWO = 1024
N_ROW = 4
N_COL = 4


def set_ends(array, own_key, least, largest):
    dims = array.shape
    spot = [jax.random.randint(jax.random.fold_in(own_key, axis), (), 0, dims[axis]) for axis in range(len(dims))]
    array = array.at[tuple(spot)].set(least)
    longest = dims.index(max(dims))
    spot[longest] = (spot[longest] + 1) % dims[longest]
    return array.at[tuple(spot)].set(largest)


def shard_levels(stream_key, dims, pieces, smallest, high):
    gain, own = 1.0, jax.random.fold_in(stream_key, 6)
    for position, parts in pieces:
        steps = jnp.exp(jax.random.uniform(jax.random.fold_in(own, position), (parts,), jnp.float32, smallest / len(pieces), high / len(pieces)))
        gain = gain * jnp.repeat(steps, dims[position] // parts).reshape([-1 if axis == position else 1 for axis in range(len(dims))])
    return gain


def routed_block(stream_key, own, number, rows, number_of, top, most, lean):
    sequence = jax.random.permutation(stream_key, number_of)
    packed, usual = shares(number_of, rows * top, most, lean, True), shares(number_of, rows * top, most, lean, False)
    places = jnp.arange(number_of)

    def named(sizes, offset_by):
        used = int((sizes > 0).sum())
        fixed = max(1, used // 4)
        passed = fixed + (places - fixed + offset_by * (used - fixed)) % max(1, number_of - fixed)
        return jnp.zeros((number_of,), jnp.int32).at[sequence[jnp.where(places < fixed, places, passed)]].set(jnp.asarray(sizes, jnp.int32))

    sizes = jnp.where(number % 4 == 0, named(packed, number // 4), named(usual, number - number // 4 - 1))
    mixed = jax.random.permutation(jax.random.fold_in(own, 3), number_of)
    donor, taker = mixed[0:number_of // 2 * 2:2], mixed[1:number_of // 2 * 2:2]
    room = jnp.minimum(sizes[donor] - 1, most - sizes[taker]) // 2
    room = jnp.where((donor == sequence[0]) | (taker == sequence[0]) | (sizes[taker] == 0), 0, jnp.maximum(room, 0))
    passed = jax.random.randint(jax.random.fold_in(own, 4), (number_of // 2,), 0, 1 << 20) % (room + 1)
    sizes = sizes.at[donor].add(-passed).at[taker].add(passed)
    items = jnp.searchsorted(jnp.cumsum(sizes), jnp.arange(rows * top), side="right").astype(jnp.int32)
    table = items.reshape(top, rows).T
    table = table[jax.random.permutation(jax.random.fold_in(own, 1), rows)]
    offset_by = jax.random.randint(jax.random.fold_in(own, 2), (rows, 1), 0, top)
    return jnp.take_along_axis(table, (jnp.arange(top)[None, :] + offset_by) % top, axis=1)


def shares(count, total, reach, lean, full):
    portions = [(1 << 20) // math.isqrt(standing ** lean) + 1 for standing in range(1, count + 1)]
    largest = reach if full else min(reach, max(-(-total // count), total * portions[0] // sum(portions)))
    least = 1 if total - largest >= count - 1 else 0
    holding, surplus = [largest] + [least] * (count - 1), total - largest - least * (count - 1)
    while surplus > 0:
        candidates = [i for i in range(1, count) if holding[i] < largest] or [i for i in range(1, count) if holding[i] < reach]
        whole, left = sum([portions[i] for i in candidates]), surplus
        for i in candidates:
            addition = min(reach - holding[i], max(1, left * portions[i] // whole), surplus)
            holding[i] = holding[i] + addition
            surplus = surplus - addition
    return np.array(holding)


def centred(rng, shape, scale, bound, kind=jnp.bfloat16):
    values = scale * jax.random.normal(rng, shape, jnp.float32)
    return jnp.clip(values, min=-bound, max=bound).astype(kind)


def setup_inputs(seed: int = 0) -> dict:
    key_of = jax.random.split(jax.random.key(seed), 7)
    parcel_patch = jnp.clip(jnp.exp(math.log(1.0) - 2.3025851 * jax.random.uniform(key_of[0], (STACK_CHIPS, PARCELS, PATCH_AREA), jnp.float32) ** shard_levels(key_of[0], (STACK_CHIPS, PARCELS, PATCH_AREA), ((0, 2), (1, 16)), -0.2, 0.2)), 0.1, 1.0)
    target_unit_keys = jax.random.split(jax.random.fold_in(key_of[1], 1), STACK_CHIPS * PARCELS // PARCELS_PER_UNIT)
    target_unit_turns = jax.random.permutation(jax.random.fold_in(key_of[1], 3), STACK_CHIPS * PARCELS // PARCELS_PER_UNIT)
    target_unit = jax.vmap(lambda own, number: routed_block(jax.random.fold_in(key_of[1], 2), own, number, PARCELS_PER_UNIT, N_ROW * N_COL, 1, PARCEL_LIMIT, 2))(target_unit_keys, target_unit_turns).reshape((STACK_CHIPS, PARCELS, 1))
    target_patch = set_ends(jax.random.randint(key_of[2], (STACK_CHIPS, PARCELS), 0, PARCELS_PER_UNIT), jax.random.fold_in(key_of[2], 1), 0, PARCELS_PER_UNIT - 1).astype(jnp.int32)
    across_taps = centred(key_of[3], (KERNEL_MODES, TAPS), TAPS ** -0.5, 0.375, jnp.float32)
    down_taps = centred(key_of[4], (KERNEL_MODES, TAPS), TAPS ** -0.5, 0.375, jnp.float32)
    source_heated_mixing = centred(key_of[5], (KERNEL_MODES, STACK_CHIPS, STACK_CHIPS), 0.4, 2.4, jnp.float32)
    return dict(parcel_patch=parcel_patch, target_unit=target_unit, target_patch=target_patch, across_taps=across_taps, down_taps=down_taps, source_heated_mixing=source_heated_mixing)


def correlate(source, kernel_taps, along):
    moved_axis = jnp.moveaxis(source, along, -1)
    length = moved_axis.shape[-1]
    tap_count = kernel_taps.shape[0]
    margin = (tap_count - 1) // 2
    extent = length + tap_count - 1
    spectrum = jnp.fft.rfft(moved_axis, extent, axis=-1) * jnp.fft.rfft(kernel_taps[::-1], extent)
    full_corr = jnp.fft.irfft(spectrum, extent, axis=-1)
    return jnp.moveaxis(full_corr[..., margin:margin + length], -1, along)


def reference(parcel_patch, target_unit, target_patch, across_taps, down_taps, source_heated_mixing):
    mesh_amount_name = N_ROW * N_COL
    tile_index = (target_unit[:, :, 0] * PARCELS_PER_UNIT + target_patch).astype(jnp.int32)
    layer_lines = jnp.arange(STACK_CHIPS, dtype=jnp.int32)[:, None]
    patch_totals_acc = jnp.zeros((STACK_CHIPS, mesh_amount_name * PARCELS_PER_UNIT, PATCH_SIDE * PATCH_SIDE), jnp.float32)
    patch_totals_acc = patch_totals_acc.at[layer_lines, tile_index].add(parcel_patch)
    mesh_layout = patch_totals_acc.reshape(STACK_CHIPS, N_ROW, N_COL, UNIT_MESH_X // PATCH_SIDE, UNIT_MESH_Y // PATCH_SIDE, PATCH_SIDE, PATCH_SIDE)
    wattage_field = mesh_layout.transpose(0, 1, 3, 5, 2, 4, 6).reshape(STACK_CHIPS, CELLS_ALONG_ONE, CELLS_ALONG_TWO)
    chip_heat_increase = jnp.zeros((STACK_CHIPS, CELLS_ALONG_ONE, CELLS_ALONG_TWO), jnp.float32)
    for warmth_addend_ordinal in range(KERNEL_MODES):
        warmth_portion = correlate(correlate(wattage_field, across_taps[warmth_addend_ordinal], 1), down_taps[warmth_addend_ordinal], 2)
        chip_heat_increase = chip_heat_increase + jnp.einsum("mu,ung->mng", source_heated_mixing[warmth_addend_ordinal], warmth_portion, precision=lax.Precision.HIGHEST)
    hottest_backward_initial = jax.nn.sigmoid(chip_heat_increase)
    adjoint_field_map = jnp.zeros((STACK_CHIPS, CELLS_ALONG_ONE, CELLS_ALONG_TWO), jnp.float32)
    for warmth_addend_ordinal in range(KERNEL_MODES):
        response = correlate(correlate(hottest_backward_initial, across_taps[warmth_addend_ordinal][::-1], 1), down_taps[warmth_addend_ordinal][::-1], 2)
        adjoint_field_map = adjoint_field_map + jnp.einsum("de,dxy->exy", source_heated_mixing[warmth_addend_ordinal], response, precision=lax.Precision.HIGHEST)
    adjoint_layout = adjoint_field_map.reshape(STACK_CHIPS, N_ROW, UNIT_MESH_X // PATCH_SIDE, PATCH_SIDE, N_COL, UNIT_MESH_Y // PATCH_SIDE, PATCH_SIDE)
    adjoint_patches = adjoint_layout.transpose(0, 1, 4, 2, 5, 3, 6).reshape(STACK_CHIPS, mesh_amount_name * PARCELS_PER_UNIT, PATCH_SIDE * PATCH_SIDE)
    block_power_slopes = adjoint_patches[layer_lines, tile_index]
    return chip_heat_increase, block_power_slopes
```

```python
import functools

import jax
import jax.numpy as jnp
from jax import lax
from jax.experimental import pallas as pl
from jax.experimental.pallas import tpu as pltpu
from jax.sharding import PartitionSpec as P

PATCH_SIDE = 16
UNIT_MESH_X = 128
UNIT_MESH_Y = 256
HALO = 128
MESH = pl.DeviceIdType.MESH


def two_halves(values):
    head = values.astype(jnp.bfloat16)
    return head, (values - head.astype(jnp.float32)).astype(jnp.bfloat16)


def dot(left, right):
    return jnp.dot(left, right, preferred_element_type=jnp.float32)


def iota(shape, dim):
    return lax.broadcasted_iota(jnp.int32, shape, dim)


def exchange_blocks(x):
    rows = x.shape[0]
    left = x[:, :128].reshape(rows // 16, 2, 8, 128)
    right = x[:, 128:].reshape(rows // 16, 2, 8, 128)
    parts = [[left[:, 0], right[:, 0]], [left[:, 1], right[:, 1]]]
    parts[0][1], parts[1][0] = parts[1][0], parts[0][1]
    line, lane = iota((1, 8, 128), 1), iota((1, 8, 128), 2)

    def inner(v):
        for bit in range(3):
            d, w = 1 << bit, 16 << bit
            low_line, low_lane = (line & d) == 0, (lane & w) == 0
            first = pltpu.roll(pltpu.roll(v, 8 - d, 1), w, 2)
            second = first if bit == 2 else pltpu.roll(pltpu.roll(v, d, 1), 128 - w, 2)
            v = jnp.where(low_line == low_lane, v, jnp.where(low_line, first, second))
        return v

    columns = [
        jnp.stack([inner(parts[0][c]), inner(parts[1][c])], axis=1).reshape(rows, 128)
        for c in range(2)
    ]
    return jnp.concatenate(columns, axis=1)


def kernel(
    patch_ref, unit_ref, tile_ref, across_ref, down_ref, mix_ref, heat_ref, slopes_ref,
    outgoing, arrived, answers, returned, label_out, label_in,
    place_keep, chosen_keep, pads, a_own, a_halo, d_cat, p_own, p_halo, y_own, x_cat,
    acc, got, swap_send, swap_recv, label_send, label_recv, halo_send, halo_recv, die_send, die_recv,
):
    here, blocks, cells = patch_ref.shape
    terms = across_ref.shape[0]
    peers, capacity = outgoing.shape[1], outgoing.shape[2]
    slots = peers * capacity
    a, b, h = UNIT_MESH_X, UNIT_MESH_Y, HALO
    tiles = (a // PATCH_SIDE) * (b // PATCH_SIDE)
    row, col, die = lax.axis_index("row"), lax.axis_index("col"), lax.axis_index("die")
    rows_mesh, cols_mesh = lax.axis_size("row"), lax.axis_size("col")
    me = row * cols_mesh + col
    has_up, has_down = row > 0, row < rows_mesh - 1
    has_left, has_right = col > 0, col < cols_mesh - 1
    up, down, left, right = {"row": row - 1}, {"row": row + 1}, {"col": col - 1}, {"col": col + 1}
    other = {"die": 1 - die}

    def place_of(number):
        return {"row": number // cols_mesh, "col": number % cols_mesh}

    pads[...] = jnp.zeros_like(pads)
    barrier = pltpu.get_barrier_semaphore()

    def greet(i, carry):
        pl.semaphore_signal(barrier, inc=1, device_id=place_of((me + i) % peers), device_id_type=MESH)
        return carry

    lax.fori_loop(1, peers, greet, 0)
    pl.semaphore_signal(barrier, inc=1, device_id=other, device_id_type=MESH)

    eye = iota((blocks, blocks), 0) == iota((blocks, blocks), 1)
    before = (iota((blocks, blocks), 1) < iota((blocks, blocks), 0)).astype(jnp.bfloat16)
    lanes = iota((blocks, blocks), 1).astype(jnp.float32)
    slot_lane = iota((blocks, slots), 1).astype(jnp.float32)
    slot_line = iota((slots, blocks), 0).astype(jnp.float32)
    labels, outs = [], []
    for k in range(here):
        dest_row = unit_ref[k : k + 1, :].astype(jnp.float32)
        dest = jnp.sum(jnp.where(eye, dest_row, 0.0), axis=1, keepdims=True)
        named = (dest == lanes).astype(jnp.bfloat16)
        count = dot(before, named)
        position = jnp.sum(named.astype(jnp.float32) * count, axis=1, keepdims=True)
        slot = dest * capacity + position
        place = (slot == slot_lane).astype(jnp.bfloat16)
        place_keep[k] = place
        slot_row = jnp.sum(jnp.where(eye, slot, 0.0), axis=0, keepdims=True)
        place_t = (slot_line == slot_row).astype(jnp.bfloat16)
        head, rest = two_halves(patch_ref[k])
        out = dot(
            jnp.concatenate([place_t, place_t], axis=1), jnp.concatenate([head, rest], axis=0)
        )
        for p in range(peers):
            outgoing[k, p] = out[p * capacity : (p + 1) * capacity]
        tile_row = (tile_ref[k : k + 1, :] + 1).astype(jnp.float32)
        tile_rows = jnp.broadcast_to(tile_row, (16, blocks)).astype(jnp.bfloat16)
        labels.append(dot(tile_rows, place)[0:1])

    slot_row_lane = iota((1, slots), 1)
    mine = jnp.logical_and(slot_row_lane >= me * capacity, slot_row_lane < (me + 1) * capacity)

    def label_rows(p, carry):
        shift = lax.rem((me - p + peers) * capacity, slots)
        rows = [jnp.where(mine, pltpu.roll(x, shift, 1), 0.0) for x in labels]
        label_out[p] = jnp.concatenate(rows, axis=1)
        return carry

    lax.fori_loop(0, peers, label_rows, 0)
    pl.semaphore_wait(barrier, peers)

    def swap_copy(stage, k, i):
        to = (me + i) % peers
        src, dst = (outgoing, arrived) if stage == 0 else (answers, returned)
        return pltpu.make_async_remote_copy(
            src_ref=src.at[k, to], dst_ref=dst.at[k, me],
            send_sem=swap_send.at[stage, k, i], recv_sem=swap_recv.at[stage, k, i],
            device_id=place_of(to), device_id_type=MESH,
        )

    def label_copy(i):
        to = (me + i) % peers
        return pltpu.make_async_remote_copy(
            src_ref=label_out.at[to], dst_ref=label_in.at[me],
            send_sem=label_send.at[i], recv_sem=label_recv.at[i],
            device_id=place_of(to), device_id_type=MESH,
        )

    def each(make, act):
        def body(j, carry):
            getattr(make((j + peers // 2 - 2) % (peers - 1) + 1), act)()
            return carry

        lax.fori_loop(1, peers, body, 0)

    def swap_each(stage, k, act):
        each(functools.partial(swap_copy, stage, k), act)

    def flat(ref, k):
        if capacity % 8 == 0:
            return ref[k].reshape(slots, cells)
        return jnp.concatenate([ref[k, p] for p in range(peers)], axis=0)

    each(label_copy, "start")
    for k in range(here):
        swap_each(0, k, "start")
    label_in[me] = label_out[me]
    for k in range(here):
        arrived[k, me] = outgoing[k, me]

    u0, u1 = iota((across_ref.shape[1], 3 * h), 0), iota((across_ref.shape[1], 3 * h), 1)
    taps = across_ref.shape[1]

    def base(taps_ref, flipped):
        pick = (u1 == (taps - u0 if flipped else u0 + 1)).astype(jnp.float32)
        return jnp.dot(
            taps_ref[...], pick, precision=lax.Precision.HIGHEST, preferred_element_type=jnp.float32
        )

    none = jnp.zeros((h, h), jnp.bfloat16)
    for stage in range(2):
        across_base = base(across_ref, stage == 1)
        down_base = base(down_ref, stage == 0)
        for t in range(terms):
            lines = pl.ds(t * a, a)
            span = jnp.broadcast_to(across_base[t : t + 1, :], (a, 3 * h))
            head, rest = two_halves(pltpu.roll(span, 0, 1, stride=1, stride_axis=0))
            for part, piece in enumerate((head, head, rest)):
                a_own[stage, lines, part * a : (part + 1) * a] = piece[:, h : 2 * h]
                a_halo[stage, lines, part * 2 * h : part * 2 * h + h] = piece[:, :h]
                a_halo[stage, lines, part * 2 * h + h : (part + 1) * 2 * h] = piece[:, 2 * h :]
            wide = jnp.broadcast_to(down_base[t : t + 1, :], (3 * h, 3 * h))
            wide = pltpu.roll(wide, h, 1, stride=1, stride_axis=0)[:, :h]
            w = b + 2 * h
            for part, piece in enumerate(two_halves(wide)):
                at = part * w
                d_cat[stage, t, at : at + b, 0:h] = piece[h : 3 * h]
                d_cat[stage, t, at : at + b, h:b] = piece[0:b]
                d_cat[stage, t, at + b : at + b + h, 0:h] = piece[0:h]
                d_cat[stage, t, at + b : at + b + h, h:b] = none
                d_cat[stage, t, at + b + h : at + w, 0:h] = none
                d_cat[stage, t, at + b + h : at + w, h:b] = piece[2 * h :]

    tops, sizes = (0, h, h + a), (h, a, h)

    def halo(stage, k, number):
        def block(band, start, width):
            return pads.at[stage, k, pl.ds(tops[band], sizes[band]), pl.ds(start, width)]

        if number == 0:
            src, dst, device = block(1, h, b), block(2, h, b), up
        elif number == 1:
            src, dst, device = block(1, h, b), block(0, h, b), down
        elif number < 5:
            src, dst, device = block(number - 2, h, h), block(number - 2, h + b, h), left
        else:
            src, dst, device = block(number - 5, b, h), block(number - 5, 0, h), right
        return pltpu.make_async_remote_copy(
            src_ref=src, dst_ref=dst,
            send_sem=halo_send.at[stage, k, number], recv_sem=halo_recv.at[stage, k, number],
            device_id=device, device_id_type=MESH,
        )

    rows_of = (has_up, None, has_down)

    def both(x, y):
        return y if x is None else jnp.logical_and(x, y)

    sends = [has_up, has_down] + [both(r, has_left) for r in rows_of] + [both(r, has_right) for r in rows_of]
    gets = [has_down, has_up] + [both(r, has_right) for r in rows_of] + [both(r, has_left) for r in rows_of]

    def act(stage, k, number, what):
        @pl.when(gets[number] if what == "wait_recv" else sends[number])
        def _():
            getattr(halo(stage, k, number), what)()

    def begin_halo(stage, k, field):
        pads[stage, k, h : h + a, h : h + b] = field
        for number in (0, 1, 3, 6):
            act(stage, k, number, "start")

    def forward(stage, k):
        act(stage, k, 0, "wait_recv")
        for number in (4, 7):
            act(stage, k, number, "start")
        act(stage, k, 1, "wait_recv")
        for number in (2, 5):
            act(stage, k, number, "start")

    def fill(stage, k, band, source, at, width):
        head, rest = two_halves(pads[stage, k, tops[band] : tops[band] + sizes[band], source : source + width])
        cols = slice(at, at + width)
        if band == 1:
            for part, piece in enumerate((head, rest, head)):
                p_own[k, part * a : (part + 1) * a, cols] = piece
        else:
            off = 0 if band == 0 else h
            for part, piece in enumerate((head, rest, head)):
                p_halo[k, part * 2 * h + off : part * 2 * h + off + h, cols] = piece

    def own_rows(stage, k, at):
        cols = slice(at, at + b)
        y_own[k, :, cols] = dot(a_own[stage], p_own[k, :, cols])

    def far_rows(stage, k, at):
        cols = slice(at, at + b)
        total = dot(a_halo[stage], p_halo[k, :, cols]) + y_own[k, :, cols]
        head, rest = two_halves(total)
        x_cat[k, :, cols] = head
        x_cat[k, :, at + b + 2 * h : at + 2 * b + 2 * h] = rest

    def along(stage, k):
        w = b + 2 * h

        def body(t, carry):
            lines = pl.ds(pl.multiple_of(t * a, a), a)
            head, rest = x_cat[k, lines, :w], x_cat[k, lines, w:]
            d_head, d_rest = d_cat[stage, t, :w], d_cat[stage, t, w:]
            z = dot(
                jnp.concatenate([head, head, rest], axis=1),
                jnp.concatenate([d_head, d_rest, d_head], axis=0),
            )
            source = die * here + k
            for d in range(2 * here):
                target = ((1 - die) if d < here else die) * here + d % here
                weight = mix_ref[t, target, source] if stage == 0 else mix_ref[t, source, target]
                acc[stage, d] = acc[stage, d] + weight * z
            return carry

        lax.fori_loop(0, terms, body, 0)

    def share(stage, k):
        return pltpu.make_async_remote_copy(
            src_ref=acc.at[stage, k], dst_ref=got.at[stage, k],
            send_sem=die_send.at[stage, k], recv_sem=die_recv.at[stage, k],
            device_id=other, device_id_type=MESH,
        )

    def run_stage(stage):
        for k in range(here):
            forward(stage, k)
            for band in (0, 2):
                fill(stage, k, band, h, 0, b)
            far_rows(stage, k, 0)
        for k in range(here):
            for number in (3, 6):
                act(stage, k, number, "wait_recv")
            fill(stage, k, 1, 0, b, h)
            fill(stage, k, 1, h + b, b + h, h)
            own_rows(stage, k, b)
            for number in (2, 4, 5, 7):
                act(stage, k, number, "wait_recv")
            for band in (0, 2):
                fill(stage, k, band, 0, b, h)
                fill(stage, k, band, h + b, b + h, h)
            far_rows(stage, k, b)
            along(stage, k)
        for k in range(here):
            share(stage, k).start()

    acc[...] = jnp.zeros_like(acc)
    each(label_copy, "wait_recv")
    label_all = jnp.sum(label_in[...], axis=0)
    tile_line = (iota((tiles, slots), 0) + 1).astype(jnp.float32)
    tile_lane = (iota((slots, tiles), 1) + 1).astype(jnp.float32)
    eye_slots = iota((slots, slots), 0) == iota((slots, slots), 1)
    for k in range(here):
        label = label_all[:, k * slots : (k + 1) * slots]
        chosen_t = (tile_line == label).astype(jnp.bfloat16)
        label_col = jnp.sum(jnp.where(eye_slots, label, 0.0), axis=1, keepdims=True)
        chosen_keep[k] = (tile_lane == label_col).astype(jnp.bfloat16)
        swap_each(0, k, "wait_recv")
        head, rest = two_halves(flat(arrived, k))
        totals = dot(
            jnp.concatenate([chosen_t, chosen_t], axis=1), jnp.concatenate([head, rest], axis=0)
        )
        begin_halo(0, k, exchange_blocks(totals))
        fill(0, k, 1, h, 0, b)
        own_rows(0, k, 0)
    run_stage(0)
    for k in range(here):
        share(0, k).wait_recv()
        heat = acc[0, here + k] + got[0, k]
        heat_ref[k] = heat
        begin_halo(1, k, jax.nn.sigmoid(heat))
        fill(1, k, 1, h, 0, b)
        own_rows(1, k, 0)
    run_stage(1)
    for k in range(here):
        share(1, k).wait_recv()
        patches = exchange_blocks(acc[1, here + k] + got[1, k])
        head, rest = two_halves(patches)
        chosen = chosen_keep[k]
        answer = dot(jnp.concatenate([chosen, chosen], axis=1), jnp.concatenate([head, rest], axis=0))
        for p in range(peers):
            answers[k, p] = answer[p * capacity : (p + 1) * capacity]
        swap_each(1, k, "start")
        returned[k, me] = answers[k, me]
    for stage in range(2):
        for k in range(here):
            for number in range(8):
                act(stage, k, number, "wait_send")
            share(stage, k).wait_send()
    each(label_copy, "wait_send")
    for k in range(here):
        swap_each(0, k, "wait_send")
    for k in range(here):
        swap_each(1, k, "wait_recv")
        head, rest = two_halves(flat(returned, k))
        place = place_keep[k]
        slopes_ref[k] = dot(
            jnp.concatenate([place, place], axis=1), jnp.concatenate([head, rest], axis=0)
        )
    for k in range(here):
        swap_each(1, k, "wait_send")


def local(parcel_patch, target_unit, target_patch, across_taps, down_taps, source_heated_mixing):
    here, blocks, cells = parcel_patch.shape
    terms, dies, _ = source_heated_mixing.shape
    peers = lax.axis_size(("row", "col"))
    capacity = max(2, 2 * blocks // peers)
    slots = peers * capacity
    a, b, h = UNIT_MESH_X, UNIT_MESH_Y, HALO
    w0, w1 = a + 2 * h, b + 2 * h
    vmem = pl.BlockSpec(memory_space=pltpu.VMEM)
    f32, bf16 = jnp.float32, jnp.bfloat16
    swap_buffer = pltpu.VMEM((here, peers, capacity, cells), f32)
    sems = pltpu.SemaphoreType.DMA
    return pl.pallas_call(
        kernel,
        out_shape=(
            jax.ShapeDtypeStruct((here, a, b), f32),
            jax.ShapeDtypeStruct((here, blocks, cells), f32),
        ),
        in_specs=[vmem] * 5 + [pl.BlockSpec(memory_space=pltpu.SMEM)],
        out_specs=(vmem, vmem),
        scratch_shapes=[
            swap_buffer, swap_buffer, swap_buffer, swap_buffer,
            pltpu.VMEM((peers, 1, here * slots), f32),
            pltpu.VMEM((peers, 1, here * slots), f32),
            pltpu.VMEM((here, blocks, slots), bf16),
            pltpu.VMEM((here, slots, (a // PATCH_SIDE) * (b // PATCH_SIDE)), bf16),
            pltpu.VMEM((2, here, w0, w1), f32),
            pltpu.VMEM((2, terms * a, 3 * a), bf16),
            pltpu.VMEM((2, terms * a, 6 * h), bf16),
            pltpu.VMEM((2, terms, 2 * w1, b), bf16),
            pltpu.VMEM((here, 3 * a, w1), bf16),
            pltpu.VMEM((here, 6 * h, w1), bf16),
            pltpu.VMEM((here, terms * a, w1), f32),
            pltpu.VMEM((here, terms * a, 2 * w1), bf16),
            pltpu.VMEM((2, dies, a, b), f32),
            pltpu.VMEM((2, here, a, b), f32),
            sems((2, here, peers)), sems((2, here, peers)),
            sems((peers,)), sems((peers,)),
            sems((2, here, 8)), sems((2, here, 8)),
            sems((2, here)), sems((2, here)),
        ],
        compiler_params=pltpu.CompilerParams(
            collective_id=0, has_side_effects=True, vmem_limit_bytes=56 * 2**20
        ),
    )(
        parcel_patch, target_unit.reshape(here, blocks), target_patch,
        across_taps, down_taps, source_heated_mixing,
    )


def solution(mesh):
    placed = (
        P("die", ("row", "col"), None),
        P("die", ("row", "col"), None),
        P("die", ("row", "col")),
        P(),
        P(),
        P(),
    )
    return jax.shard_map(
        local,
        mesh=mesh,
        in_specs=placed,
        out_specs=(P("die", "row", "col"), P("die", ("row", "col"), None)),
        check_vma=False,
    )
```

```python
import functools

import jax
import jax.numpy as jnp
from jax import lax
from jax.experimental import pallas as pl
from jax.experimental.pallas import tpu as pltpu
from jax.sharding import PartitionSpec as P

PATCH_SIDE = 16
UNIT_MESH_X = 128
UNIT_MESH_Y = 256
HALO = 128
MESH = pl.DeviceIdType.MESH


def two_halves(values):
    head = values.astype(jnp.bfloat16)
    return head, (values - head.astype(jnp.float32)).astype(jnp.bfloat16)


def dot(left, right):
    return jnp.dot(left, right, preferred_element_type=jnp.float32)


def iota(shape, dim):
    return lax.broadcasted_iota(jnp.int32, shape, dim)


def exchange_blocks(x):
    rows = x.shape[0]
    left = x[:, :128].reshape(rows // 16, 2, 8, 128)
    right = x[:, 128:].reshape(rows // 16, 2, 8, 128)
    parts = [[left[:, 0], right[:, 0]], [left[:, 1], right[:, 1]]]
    parts[0][1], parts[1][0] = parts[1][0], parts[0][1]
    line, lane = iota((1, 8, 128), 1), iota((1, 8, 128), 2)

    def inner(v):
        for bit in range(3):
            d, w = 1 << bit, 16 << bit
            low_line, low_lane = (line & d) == 0, (lane & w) == 0
            first = pltpu.roll(pltpu.roll(v, 8 - d, 1), w, 2)
            second = first if bit == 2 else pltpu.roll(pltpu.roll(v, d, 1), 128 - w, 2)
            v = jnp.where(low_line == low_lane, v, jnp.where(low_line, first, second))
        return v

    columns = [
        jnp.stack([inner(parts[0][c]), inner(parts[1][c])], axis=1).reshape(rows, 128)
        for c in range(2)
    ]
    return jnp.concatenate(columns, axis=1)


def kernel(
    patch_ref, unit_ref, tile_ref, across_ref, down_ref, mix_ref, heat_ref, slopes_ref,
    outgoing, arrived, answers, returned, label_out, label_in,
    place_keep, chosen_keep, pads, a_own, a_halo, d_cat, p_own, p_halo, y_own, x_cat,
    acc, got, swap_send, swap_recv, label_send, label_recv, halo_send, halo_recv, die_send, die_recv,
):
    here, blocks, cells = patch_ref.shape
    terms = across_ref.shape[0]
    peers, capacity = outgoing.shape[1], outgoing.shape[2]
    slots = peers * capacity
    a, b, h = UNIT_MESH_X, UNIT_MESH_Y, HALO
    tiles = (a // PATCH_SIDE) * (b // PATCH_SIDE)
    row, col, die = lax.axis_index("row"), lax.axis_index("col"), lax.axis_index("die")
    rows_mesh, cols_mesh = lax.axis_size("row"), lax.axis_size("col")
    me = row * cols_mesh + col
    has_up, has_down = row > 0, row < rows_mesh - 1
    has_left, has_right = col > 0, col < cols_mesh - 1
    up, down, left, right = {"row": row - 1}, {"row": row + 1}, {"col": col - 1}, {"col": col + 1}
    other = {"die": 1 - die}

    def place_of(number):
        return {"row": number // cols_mesh, "col": number % cols_mesh}

    barrier = pltpu.get_barrier_semaphore()

    def greet(i, carry):
        pl.semaphore_signal(barrier, inc=1, device_id=place_of((me + i) % peers), device_id_type=MESH)
        return carry

    lax.fori_loop(1, peers, greet, 0)
    pl.semaphore_signal(barrier, inc=1, device_id=other, device_id_type=MESH)

    eye = iota((blocks, blocks), 0) == iota((blocks, blocks), 1)
    before = (iota((blocks, blocks), 1) < iota((blocks, blocks), 0)).astype(jnp.bfloat16)
    lanes = iota((blocks, blocks), 1).astype(jnp.float32)
    slot_lane = iota((blocks, slots), 1).astype(jnp.float32)
    slot_line = iota((slots, blocks), 0).astype(jnp.float32)
    labels, outs = [], []
    for k in range(here):
        dest_row = unit_ref[k : k + 1, :].astype(jnp.float32)
        dest = jnp.sum(jnp.where(eye, dest_row, 0.0), axis=1, keepdims=True)
        named = (dest == lanes).astype(jnp.bfloat16)
        count = dot(before, named)
        position = jnp.sum(named.astype(jnp.float32) * count, axis=1, keepdims=True)
        slot = dest * capacity + position
        place = (slot == slot_lane).astype(jnp.bfloat16)
        place_keep[k] = place
        slot_row = jnp.sum(jnp.where(eye, slot, 0.0), axis=0, keepdims=True)
        place_t = (slot_line == slot_row).astype(jnp.bfloat16)
        head, rest = two_halves(patch_ref[k])
        out = dot(
            jnp.concatenate([place_t, place_t], axis=1), jnp.concatenate([head, rest], axis=0)
        )
        for p in range(peers):
            outgoing[k, p] = out[p * capacity : (p + 1) * capacity]
        tile_row = (tile_ref[k : k + 1, :] + 1).astype(jnp.float32)
        tile_rows = jnp.broadcast_to(tile_row, (16, blocks)).astype(jnp.bfloat16)
        labels.append(dot(tile_rows, place)[0:1])

    slot_row_lane = iota((1, slots), 1)
    mine = jnp.logical_and(slot_row_lane >= me * capacity, slot_row_lane < (me + 1) * capacity)

    def label_rows(p, carry):
        shift = lax.rem((me - p + peers) * capacity, slots)
        rows = [jnp.where(mine, pltpu.roll(x, shift, 1), 0.0) for x in labels]
        label_out[p] = jnp.concatenate(rows, axis=1)
        return carry

    lax.fori_loop(0, peers, label_rows, 0)
    pl.semaphore_wait(barrier, peers)

    def swap_copy(stage, k, i):
        to = (me + i) % peers
        src, dst = (outgoing, arrived) if stage == 0 else (answers, returned)
        return pltpu.make_async_remote_copy(
            src_ref=src.at[k, to], dst_ref=dst.at[k, me],
            send_sem=swap_send.at[stage, k, i], recv_sem=swap_recv.at[stage, k, i],
            device_id=place_of(to), device_id_type=MESH,
        )

    def label_copy(i):
        to = (me + i) % peers
        return pltpu.make_async_remote_copy(
            src_ref=label_out.at[to], dst_ref=label_in.at[me],
            send_sem=label_send.at[i], recv_sem=label_recv.at[i],
            device_id=place_of(to), device_id_type=MESH,
        )

    def each(make, act):
        def body(j, carry):
            getattr(make((j + peers // 2 - 2) % (peers - 1) + 1), act)()
            return carry

        lax.fori_loop(1, peers, body, 0)

    def swap_each(stage, k, act):
        each(functools.partial(swap_copy, stage, k), act)

    def flat(ref, k):
        if capacity % 8 == 0:
            return ref[k].reshape(slots, cells)
        return jnp.concatenate([ref[k, p] for p in range(peers)], axis=0)

    each(label_copy, "start")
    for k in range(here):
        swap_each(0, k, "start")
    label_in[me] = label_out[me]
    for k in range(here):
        arrived[k, me] = outgoing[k, me]

    w0, w1 = a + 2 * h, b + 2 * h
    for there, lines, cols in (
        (has_up, slice(0, h), slice(0, w1)),
        (has_down, slice(h + a, w0), slice(0, w1)),
        (has_left, slice(0, w0), slice(0, h)),
        (has_right, slice(0, w0), slice(h + b, w1)),
    ):
        @pl.when(jnp.logical_not(there))
        def _(lines=lines, cols=cols):
            part = pads[:, :, lines, cols]
            pads[:, :, lines, cols] = jnp.zeros_like(part)

    u0, u1 = iota((across_ref.shape[1], 3 * h), 0), iota((across_ref.shape[1], 3 * h), 1)
    taps = across_ref.shape[1]

    def base(taps_ref, flipped):
        pick = (u1 == (taps - u0 if flipped else u0 + 1)).astype(jnp.float32)
        return jnp.dot(
            taps_ref[...], pick, precision=lax.Precision.HIGHEST, preferred_element_type=jnp.float32
        )

    none = jnp.zeros((h, h), jnp.bfloat16)
    for stage in range(2):
        across_base = base(across_ref, stage == 1)
        down_base = base(down_ref, stage == 0)
        for t in range(terms):
            lines = pl.ds(t * a, a)
            span = jnp.broadcast_to(across_base[t : t + 1, :], (a, 3 * h))
            head, rest = two_halves(pltpu.roll(span, 0, 1, stride=1, stride_axis=0))
            for part, piece in enumerate((head, head, rest)):
                a_own[stage, lines, part * a : (part + 1) * a] = piece[:, h : 2 * h]
                a_halo[stage, lines, part * 2 * h : part * 2 * h + h] = piece[:, :h]
                a_halo[stage, lines, part * 2 * h + h : (part + 1) * 2 * h] = piece[:, 2 * h :]
            wide = jnp.broadcast_to(down_base[t : t + 1, :], (3 * h, 3 * h))
            wide = pltpu.roll(wide, h, 1, stride=1, stride_axis=0)[:, :h]
            w = b + 2 * h
            for part, piece in enumerate(two_halves(wide)):
                at = part * w
                d_cat[stage, t, at : at + b, 0:h] = piece[h : 3 * h]
                d_cat[stage, t, at : at + b, h:b] = piece[0:b]
                d_cat[stage, t, at + b : at + b + h, 0:h] = piece[0:h]
                d_cat[stage, t, at + b : at + b + h, h:b] = none
                d_cat[stage, t, at + b + h : at + w, 0:h] = none
                d_cat[stage, t, at + b + h : at + w, h:b] = piece[2 * h :]

    tops, sizes, half = (0, h, h + a), (h, a, h), a // 2

    def halo(stage, k, number):
        def block(band, start, width, part=None):
            lines = pl.ds(tops[band], sizes[band]) if part is None else pl.ds(tops[band] + part * half, half)
            return pads.at[stage, k, lines, pl.ds(start, width)]

        if number in (0, 8):
            src, dst, device = block(1, h, b, number // 8), block(2, h, b, number // 8), up
        elif number in (1, 9):
            src, dst, device = block(1, h, b, number // 8), block(0, h, b, number // 8), down
        elif number < 5:
            src, dst, device = block(number - 2, h, h), block(number - 2, h + b, h), left
        else:
            src, dst, device = block(number - 5, b, h), block(number - 5, 0, h), right
        return pltpu.make_async_remote_copy(
            src_ref=src, dst_ref=dst,
            send_sem=halo_send.at[stage, k, number], recv_sem=halo_recv.at[stage, k, number],
            device_id=device, device_id_type=MESH,
        )

    rows_of = (has_up, None, has_down)

    def both(x, y):
        return y if x is None else jnp.logical_and(x, y)

    sends = [has_up, has_down] + [both(r, has_left) for r in rows_of] + [both(r, has_right) for r in rows_of]
    sends = sends + sends[:2]
    gets = [has_down, has_up] + [both(r, has_right) for r in rows_of] + [both(r, has_left) for r in rows_of]
    gets = gets + gets[:2]

    def act(stage, k, number, what):
        @pl.when(gets[number] if what == "wait_recv" else sends[number])
        def _():
            getattr(halo(stage, k, number), what)()

    def begin_halo(stage, k, field, part):
        pads[stage, k, h + part * half : h + (part + 1) * half, h : h + b] = field
        for number in (8 * part, 8 * part + 1) + ((3, 6) if part == 1 else ()):
            act(stage, k, number, "start")

    def forward(stage, k):
        for from_down, corners in ((0, (4, 7)), (1, (2, 5))):
            for part in range(2):
                act(stage, k, from_down + 8 * part, "wait_recv")
            for number in corners:
                act(stage, k, number, "start")

    def fill(stage, k, band, source, at, width):
        head, rest = two_halves(pads[stage, k, tops[band] : tops[band] + sizes[band], source : source + width])
        cols = slice(at, at + width)
        if band == 1:
            for part, piece in enumerate((head, rest, head)):
                p_own[k, part * a : (part + 1) * a, cols] = piece
        else:
            off = 0 if band == 0 else h
            for part, piece in enumerate((head, rest, head)):
                p_halo[k, part * 2 * h + off : part * 2 * h + off + h, cols] = piece

    def own_rows(stage, k, at):
        cols = slice(at, at + b)
        y_own[k, :, cols] = dot(a_own[stage], p_own[k, :, cols])

    def far_rows(stage, k, at):
        cols = slice(at, at + b)
        total = dot(a_halo[stage], p_halo[k, :, cols]) + y_own[k, :, cols]
        head, rest = two_halves(total)
        x_cat[k, :, cols] = head
        x_cat[k, :, at + b + 2 * h : at + 2 * b + 2 * h] = rest

    def along(stage, k, first, last):
        w = b + 2 * h
        source = die * here + k

        def body(t, fresh):
            lines = pl.ds(pl.multiple_of(t * a, a), a)
            head, rest = x_cat[k, lines, :w], x_cat[k, lines, w:]
            d_head, d_rest = d_cat[stage, t, :w], d_cat[stage, t, w:]
            z = dot(
                jnp.concatenate([head, head, rest], axis=1),
                jnp.concatenate([d_head, d_rest, d_head], axis=0),
            )
            for d in range(2 * here):
                target = ((1 - die) if d < here else die) * here + d % here
                weight = mix_ref[target, source, t] if stage == 0 else mix_ref[source, target, t]
                acc[stage, d] = weight * z if fresh else acc[stage, d] + weight * z

        if k == 0 and first == 0:
            body(0, True)
            first = 1

        def step(t, carry):
            body(t, False)
            return carry

        lax.fori_loop(first, last, step, 0, unroll=True)

    def share(stage, k, part):
        lines = pl.ds(part * half, half)
        return pltpu.make_async_remote_copy(
            src_ref=acc.at[stage, k, lines], dst_ref=got.at[stage, k, lines],
            send_sem=die_send.at[stage, k, part], recv_sem=die_recv.at[stage, k, part],
            device_id=other, device_id_type=MESH,
        )

    def far_middle(stage, k):
        for band in (0, 2):
            fill(stage, k, band, h, 0, b)
        far_rows(stage, k, 0)

    def own_sides(stage, k):
        for number in (3, 6):
            act(stage, k, number, "wait_recv")
        fill(stage, k, 1, 0, b, h)
        fill(stage, k, 1, h + b, b + h, h)
        own_rows(stage, k, b)

    def far_sides(stage, k):
        for number in (2, 4, 5, 7):
            act(stage, k, number, "wait_recv")
        for band in (0, 2):
            fill(stage, k, band, 0, b, h)
            fill(stage, k, band, h + b, b + h, h)
        far_rows(stage, k, b)

    def run_stage(stage):
        last = here - 1
        for k in range(last):
            own_sides(stage, k)
            forward(stage, k)
            far_middle(stage, k)
            far_sides(stage, k)
            if k == last - 1:
                along(stage, k, 0, terms // 2)
                own_sides(stage, last)
                forward(stage, last)
                along(stage, k, terms // 2, terms)
            else:
                along(stage, k, 0, terms)
        far_middle(stage, last)
        far_sides(stage, last)
        along(stage, last, 0, terms)
        for k in range(here):
            for part in range(2):
                share(stage, k, part).start()

    each(label_copy, "wait_recv")
    label_all = jnp.sum(label_in[...], axis=0)
    tile_line = (iota((tiles, slots), 0) + 1).astype(jnp.float32)
    tile_lane = (iota((slots, tiles), 1) + 1).astype(jnp.float32)
    eye_slots = iota((slots, slots), 0) == iota((slots, slots), 1)
    for k in range(here):
        label = label_all[:, k * slots : (k + 1) * slots]
        chosen_t = (tile_line == label).astype(jnp.bfloat16)
        label_col = jnp.sum(jnp.where(eye_slots, label, 0.0), axis=1, keepdims=True)
        chosen_keep[k] = (tile_lane == label_col).astype(jnp.bfloat16)
        swap_each(0, k, "wait_recv")
        head, rest = two_halves(flat(arrived, k))
        totals = dot(
            jnp.concatenate([chosen_t, chosen_t], axis=1), jnp.concatenate([head, rest], axis=0)
        )
        field = exchange_blocks(totals)
        for part in range(2):
            begin_halo(0, k, field[part * half : (part + 1) * half], part)
        fill(0, k, 1, h, 0, b)
        own_rows(0, k, 0)
    run_stage(0)
    for k in range(here):
        for part in range(2):
            share(0, k, part).wait_recv()
            lines = slice(part * half, (part + 1) * half)
            heat = acc[0, here + k, lines] + got[0, k, lines]
            heat_ref[k, lines] = heat
            begin_halo(1, k, jax.nn.sigmoid(heat), part)
        fill(1, k, 1, h, 0, b)
        own_rows(1, k, 0)
    run_stage(1)
    for k in range(here):
        for part in range(2):
            share(1, k, part).wait_recv()
        patches = exchange_blocks(acc[1, here + k] + got[1, k])
        head, rest = two_halves(patches)
        chosen = chosen_keep[k]
        answer = dot(jnp.concatenate([chosen, chosen], axis=1), jnp.concatenate([head, rest], axis=0))
        for p in range(peers):
            answers[k, p] = answer[p * capacity : (p + 1) * capacity]
        swap_each(1, k, "start")
        returned[k, me] = answers[k, me]
    for stage in range(2):
        for k in range(here):
            for number in range(10):
                act(stage, k, number, "wait_send")
            for part in range(2):
                share(stage, k, part).wait_send()
    each(label_copy, "wait_send")
    for k in range(here):
        swap_each(0, k, "wait_send")
    for k in range(here):
        swap_each(1, k, "wait_recv")
        head, rest = two_halves(flat(returned, k))
        place = place_keep[k]
        slopes_ref[k] = dot(
            jnp.concatenate([place, place], axis=1), jnp.concatenate([head, rest], axis=0)
        )
    for k in range(here):
        swap_each(1, k, "wait_send")


def local(parcel_patch, target_unit, target_patch, across_taps, down_taps, source_heated_mixing):
    here, blocks, cells = parcel_patch.shape
    terms, dies, _ = source_heated_mixing.shape
    peers = lax.axis_size(("row", "col"))
    capacity = max(2, 2 * blocks // peers)
    slots = peers * capacity
    a, b, h = UNIT_MESH_X, UNIT_MESH_Y, HALO
    w0, w1 = a + 2 * h, b + 2 * h
    vmem = pl.BlockSpec(memory_space=pltpu.VMEM)
    f32, bf16 = jnp.float32, jnp.bfloat16
    swap_buffer = pltpu.VMEM((here, peers, capacity, cells), f32)
    sems = pltpu.SemaphoreType.DMA
    return pl.pallas_call(
        kernel,
        out_shape=(
            jax.ShapeDtypeStruct((here, a, b), f32),
            jax.ShapeDtypeStruct((here, blocks, cells), f32),
        ),
        in_specs=[vmem] * 5 + [pl.BlockSpec(memory_space=pltpu.SMEM)],
        out_specs=(vmem, vmem),
        scratch_shapes=[
            swap_buffer, swap_buffer, swap_buffer, swap_buffer,
            pltpu.VMEM((peers, 1, here * slots), f32),
            pltpu.VMEM((peers, 1, here * slots), f32),
            pltpu.VMEM((here, blocks, slots), bf16),
            pltpu.VMEM((here, slots, (a // PATCH_SIDE) * (b // PATCH_SIDE)), bf16),
            pltpu.VMEM((2, here, w0, w1), f32),
            pltpu.VMEM((2, terms * a, 3 * a), bf16),
            pltpu.VMEM((2, terms * a, 6 * h), bf16),
            pltpu.VMEM((2, terms, 2 * w1, b), bf16),
            pltpu.VMEM((here, 3 * a, w1), bf16),
            pltpu.VMEM((here, 6 * h, w1), bf16),
            pltpu.VMEM((here, terms * a, w1), f32),
            pltpu.VMEM((here, terms * a, 2 * w1), bf16),
            pltpu.VMEM((2, dies, a, b), f32),
            pltpu.VMEM((2, here, a, b), f32),
            sems((2, here, peers)), sems((2, here, peers)),
            sems((peers,)), sems((peers,)),
            sems((2, here, 10)), sems((2, here, 10)),
            sems((2, here, 2)), sems((2, here, 2)),
        ],
        compiler_params=pltpu.CompilerParams(
            collective_id=0, has_side_effects=True, vmem_limit_bytes=56 * 2**20
        ),
    )(
        parcel_patch, target_unit.reshape(here, blocks), target_patch,
        across_taps, down_taps, source_heated_mixing.transpose(1, 2, 0),
    )


def solution(mesh):
    placed = (
        P("die", ("row", "col"), None),
        P("die", ("row", "col"), None),
        P("die", ("row", "col")),
        P(),
        P(),
        P(),
    )
    return jax.shard_map(
        local,
        mesh=mesh,
        in_specs=placed,
        out_specs=(P("die", "row", "col"), P("die", ("row", "col"), None)),
        check_vma=False,
    )
```

```python
import functools

import jax
import jax.numpy as jnp
from jax import lax
from jax.experimental import pallas as pl
from jax.experimental.pallas import tpu as pltpu
from jax.sharding import PartitionSpec as P

PATCH_SIDE = 16
UNIT_MESH_X = 128
UNIT_MESH_Y = 256
HALO = 128
MESH = pl.DeviceIdType.MESH


def two_halves(values):
    head = values.astype(jnp.bfloat16)
    return head, (values - head.astype(jnp.float32)).astype(jnp.bfloat16)


def dot(left, right):
    return jnp.dot(left, right, preferred_element_type=jnp.float32)


def iota(shape, dim):
    return lax.broadcasted_iota(jnp.int32, shape, dim)


def exchange_blocks(x):
    rows = x.shape[0]
    left = x[:, :128].reshape(rows // 16, 2, 8, 128)
    right = x[:, 128:].reshape(rows // 16, 2, 8, 128)
    parts = [[left[:, 0], right[:, 0]], [left[:, 1], right[:, 1]]]
    parts[0][1], parts[1][0] = parts[1][0], parts[0][1]
    line, lane = iota((1, 8, 128), 1), iota((1, 8, 128), 2)

    def inner(v):
        for bit in range(3):
            d, w = 1 << bit, 16 << bit
            low_line, low_lane = (line & d) == 0, (lane & w) == 0
            first = pltpu.roll(pltpu.roll(v, 8 - d, 1), w, 2)
            second = first if bit == 2 else pltpu.roll(pltpu.roll(v, d, 1), 128 - w, 2)
            v = jnp.where(low_line == low_lane, v, jnp.where(low_line, first, second))
        return v

    columns = [
        jnp.stack([inner(parts[0][c]), inner(parts[1][c])], axis=1).reshape(rows, 128)
        for c in range(2)
    ]
    return jnp.concatenate(columns, axis=1)


def kernel(
    patch_in, unit_in, tile_in, across_in, down_in, mix_ref, heat_out, slopes_out,
    patch_ref, unit_ref, tile_ref, across_ref, down_ref, heat_ref, slopes_ref, in_sems, out_sems,
    outgoing, arrived, answers, returned, label_out, label_in, label_rows,
    place_keep, chosen_keep, pads, a_own, a_halo, d_cat, p_own, p_halo, y_own, x_cat,
    z_all, acc, got, swap_send, swap_recv, label_sems, halo_send, halo_recv, die_send, die_recv,
):
    here, blocks, cells = patch_ref.shape
    terms = across_ref.shape[0]
    peers, capacity = outgoing.shape[1], outgoing.shape[2]
    slots = peers * capacity
    a, b, h = UNIT_MESH_X, UNIT_MESH_Y, HALO
    tiles = (a // PATCH_SIDE) * (b // PATCH_SIDE)
    row, col, die = lax.axis_index("row"), lax.axis_index("col"), lax.axis_index("die")
    rows_mesh, cols_mesh = lax.axis_size("row"), lax.axis_size("col")
    me = row * cols_mesh + col
    has_up, has_down = row > 0, row < rows_mesh - 1
    has_left, has_right = col > 0, col < cols_mesh - 1
    up, down, left, right = {"row": row - 1}, {"row": row + 1}, {"col": col - 1}, {"col": col + 1}
    other = {"die": 1 - die}

    def place_of(number):
        return {"row": number // cols_mesh, "col": number % cols_mesh}

    loads = [
        pltpu.make_async_copy(src, dst, in_sems.at[i])
        for i, (src, dst) in enumerate((
            (unit_in, unit_ref), (tile_in, tile_ref), (patch_in, patch_ref),
            (across_in, across_ref), (down_in, down_ref),
        ))
    ]
    for load in loads:
        load.start()
    barrier = pltpu.get_barrier_semaphore()

    def greet(i, carry):
        pl.semaphore_signal(barrier, inc=1, device_id=place_of((me + i) % peers), device_id_type=MESH)
        return carry

    lax.fori_loop(1, peers, greet, 0)
    pl.semaphore_signal(barrier, inc=1, device_id=other, device_id_type=MESH)

    for load in loads[:3]:
        load.wait()
    eye = iota((blocks, blocks), 0) == iota((blocks, blocks), 1)
    before = (iota((blocks, blocks), 1) < iota((blocks, blocks), 0)).astype(jnp.bfloat16)
    lanes = iota((blocks, 128), 1).astype(jnp.float32)
    slot_lane = iota((blocks, slots), 1).astype(jnp.float32)
    slot_line = iota((slots, blocks), 0).astype(jnp.float32)
    peer_line = iota((peers, blocks), 0).astype(jnp.float32)

    def column(line):
        return jnp.sum(jnp.where(eye, line, 0.0), axis=1, keepdims=True)

    def route(k):
        dest_row = unit_ref[k : k + 1, :].astype(jnp.float32)
        dest = column(dest_row)
        named = (dest == lanes).astype(jnp.bfloat16)
        count = dot(before, named)
        position = jnp.sum(named.astype(jnp.float32) * count, axis=1, keepdims=True)
        slot = dest * capacity + position
        slot_row = jnp.sum(jnp.where(eye, slot, 0.0), axis=0, keepdims=True)
        place_t = (slot_line == slot_row).astype(jnp.bfloat16)
        head, rest = two_halves(patch_ref[k])
        out = dot(
            jnp.concatenate([place_t, place_t], axis=1), jnp.concatenate([head, rest], axis=0)
        )
        for p in range(peers):
            outgoing[k, p] = out[p * capacity : (p + 1) * capacity]
        return dest_row, position, slot

    def label_part(k, dest_row, position):
        tile = column((tile_ref[k : k + 1, :] + 1).astype(jnp.float32))
        spread = jnp.where(lanes == position + k * capacity, tile, 0.0).astype(jnp.bfloat16)
        return dot((peer_line == dest_row).astype(jnp.bfloat16), spread)

    def swap_copy(stage, k, i):
        to = (me + i) % peers
        src, dst = (outgoing, arrived) if stage == 0 else (answers, returned)
        return pltpu.make_async_remote_copy(
            src_ref=src.at[k, to], dst_ref=dst.at[k, me],
            send_sem=swap_send.at[stage, k], recv_sem=swap_recv.at[stage, k],
            device_id=place_of(to), device_id_type=MESH,
        )

    def swap_all(stage, k):
        src, dst = (outgoing, arrived) if stage == 0 else (answers, returned)
        return pltpu.make_async_remote_copy(
            src_ref=src.at[k, pl.ds(0, peers - 1)], dst_ref=dst.at[k, pl.ds(0, peers - 1)],
            send_sem=swap_send.at[stage, k], recv_sem=swap_recv.at[stage, k],
            device_id=other, device_id_type=MESH,
        )

    def label_copy(i):
        to = (me + i) % peers
        return pltpu.make_async_remote_copy(
            src_ref=label_out.at[to], dst_ref=label_in.at[me],
            send_sem=label_sems.at[0], recv_sem=label_sems.at[1],
            device_id=place_of(to), device_id_type=MESH,
        )

    def label_all():
        return pltpu.make_async_remote_copy(
            src_ref=label_out.at[pl.ds(0, peers - 1)], dst_ref=label_in.at[pl.ds(0, peers - 1)],
            send_sem=label_sems.at[0], recv_sem=label_sems.at[1],
            device_id=other, device_id_type=MESH,
        )

    def start_each(make):
        def body(j, carry):
            make((j + peers // 2 - 2) % (peers - 1) + 1).start()
            return carry

        lax.fori_loop(1, peers, body, 0)

    def flat(ref, k):
        if capacity % 8 == 0:
            return ref[k].reshape(slots, cells)
        return jnp.concatenate([ref[k, p] for p in range(peers)], axis=0)

    routes = [route(0)]
    pl.semaphore_wait(barrier, peers)
    start_each(functools.partial(swap_copy, 0, 0))
    routes += [route(k) for k in range(1, here)]
    label_sum = sum(label_part(k, *routes[k][:2]) for k in range(here))
    for p in range(peers):
        label_out[p] = label_sum[p : p + 1]
    start_each(label_copy)
    for k in range(1, here):
        start_each(functools.partial(swap_copy, 0, k))
    label_in[me] = label_out[me]
    for k in range(here):
        place_keep[k] = (routes[k][2] == slot_lane).astype(jnp.bfloat16)
        arrived[k, me] = outgoing[k, me]

    w0, w1 = a + 2 * h, b + 2 * h
    for there, lines, cols in (
        (has_up, slice(0, h), slice(0, w1)),
        (has_down, slice(h + a, w0), slice(0, w1)),
        (has_left, slice(0, w0), slice(0, h)),
        (has_right, slice(0, w0), slice(h + b, w1)),
    ):
        @pl.when(jnp.logical_not(there))
        def _(lines=lines, cols=cols):
            part = pads[:, :, lines, cols]
            pads[:, :, lines, cols] = jnp.zeros_like(part)

    for load in loads[3:]:
        load.wait()
    u0, u1 = iota((across_ref.shape[1], 3 * h), 0), iota((across_ref.shape[1], 3 * h), 1)
    taps = across_ref.shape[1]

    def base(taps_ref, flipped):
        pick = (u1 == (taps - u0 if flipped else u0 + 1)).astype(jnp.float32)
        return jnp.dot(
            taps_ref[...], pick, precision=lax.Precision.HIGHEST, preferred_element_type=jnp.float32
        )

    none = jnp.zeros((h, h), jnp.bfloat16)
    for stage in range(2):
        across_base = base(across_ref, stage == 1)
        down_base = base(down_ref, stage == 0)
        for t in range(terms):
            lines = pl.ds(t * a, a)
            span = jnp.broadcast_to(across_base[t : t + 1, :], (a, 3 * h))
            head, rest = two_halves(pltpu.roll(span, 0, 1, stride=1, stride_axis=0))
            for part, piece in enumerate((head, head, rest)):
                a_own[stage, lines, part * a : (part + 1) * a] = piece[:, h : 2 * h]
                a_halo[stage, lines, part * 2 * h : part * 2 * h + h] = piece[:, :h]
                a_halo[stage, lines, part * 2 * h + h : (part + 1) * 2 * h] = piece[:, 2 * h :]
            wide = jnp.broadcast_to(down_base[t : t + 1, :], (3 * h, 3 * h))
            wide = pltpu.roll(wide, h, 1, stride=1, stride_axis=0)[:, :h]
            w = b + 2 * h
            for part, piece in enumerate(two_halves(wide)):
                at = part * w
                d_cat[stage, t, at : at + b, 0:h] = piece[h : 3 * h]
                d_cat[stage, t, at : at + b, h:b] = piece[0:b]
                d_cat[stage, t, at + b : at + b + h, 0:h] = piece[0:h]
                d_cat[stage, t, at + b : at + b + h, h:b] = none
                d_cat[stage, t, at + b + h : at + w, 0:h] = none
                d_cat[stage, t, at + b + h : at + w, h:b] = piece[2 * h :]

    tops, sizes, half = (0, h, h + a), (h, a, h), a // 2

    def halo(stage, k, number):
        def block(band, start, width, part=None):
            lines = pl.ds(tops[band], sizes[band]) if part is None else pl.ds(tops[band] + part * half, half)
            return pads.at[stage, k, lines, pl.ds(start, width)]

        if number in (0, 8):
            src, dst, device = block(1, h, b, number // 8), block(2, h, b, number // 8), up
        elif number in (1, 9):
            src, dst, device = block(1, h, b, number // 8), block(0, h, b, number // 8), down
        elif number < 5:
            src, dst, device = block(number - 2, h, h), block(number - 2, h + b, h), left
        else:
            src, dst, device = block(number - 5, b, h), block(number - 5, 0, h), right
        return pltpu.make_async_remote_copy(
            src_ref=src, dst_ref=dst,
            send_sem=halo_send.at[stage, k, number], recv_sem=halo_recv.at[stage, k, number],
            device_id=device, device_id_type=MESH,
        )

    rows_of = (has_up, None, has_down)

    def both(x, y):
        return y if x is None else jnp.logical_and(x, y)

    sends = [has_up, has_down] + [both(r, has_left) for r in rows_of] + [both(r, has_right) for r in rows_of]
    sends = sends + sends[:2]
    gets = [has_down, has_up] + [both(r, has_right) for r in rows_of] + [both(r, has_left) for r in rows_of]
    gets = gets + gets[:2]

    def act(stage, k, number, what):
        @pl.when(gets[number] if what == "wait_recv" else sends[number])
        def _():
            getattr(halo(stage, k, number), what)()

    def begin_halo(stage, k, field, part):
        pads[stage, k, h + part * half : h + (part + 1) * half, h : h + b] = field
        for number in (8 * part, 8 * part + 1) + ((3, 6) if part == 1 else ()):
            act(stage, k, number, "start")

    def forward(stage, k):
        for from_down, corners in ((0, (4, 7)), (1, (2, 5))):
            for part in range(2):
                act(stage, k, from_down + 8 * part, "wait_recv")
            for number in corners:
                act(stage, k, number, "start")

    def fill(stage, k, band, source, at, width):
        head, rest = two_halves(pads[stage, k, tops[band] : tops[band] + sizes[band], source : source + width])
        cols = slice(at, at + width)
        if band == 1:
            for part, piece in enumerate((head, rest, head)):
                p_own[k, part * a : (part + 1) * a, cols] = piece
        else:
            off = 0 if band == 0 else h
            for part, piece in enumerate((head, rest, head)):
                p_halo[k, part * 2 * h + off : part * 2 * h + off + h, cols] = piece

    def own_rows(stage, k, at):
        cols = slice(at, at + b)
        y_own[k, :, cols] = dot(a_own[stage], p_own[k, :, cols])

    def far_rows(stage, k, at):
        cols = slice(at, at + b)
        total = dot(a_halo[stage], p_halo[k, :, cols]) + y_own[k, :, cols]
        head, rest = two_halves(total)
        x_cat[k, :, cols] = head
        x_cat[k, :, at + b + 2 * h : at + 2 * b + 2 * h] = rest

    def along(stage, k, at):
        w = b + 2 * h
        head_cols, rest_cols = slice(at, at + b), slice(w + at, w + at + b)

        def step(t, carry):
            lines = pl.ds(pl.multiple_of(t * a, a), a)
            head, rest = x_cat[k, lines, head_cols], x_cat[k, lines, rest_cols]
            d_head, d_rest = d_cat[stage, t, head_cols], d_cat[stage, t, rest_cols]
            z = dot(
                jnp.concatenate([head, head, rest], axis=1),
                jnp.concatenate([d_head, d_rest, d_head], axis=0),
            )
            z_all[k, t] = z if at == 0 else z_all[k, t] + z
            return carry

        lax.fori_loop(0, terms, step, 0, unroll=True)

    def mix(stage, d, part):
        target = ((1 - die) if d < here else die) * here + d % here
        weights = []
        for k in range(here):
            source = die * here + k
            for t in range(terms):
                pair = (target, source) if stage == 0 else (source, target)
                weights.append(mix_ref[pair[0], pair[1], t])

        def step(i, carry):
            lines = pl.ds(pl.multiple_of(part * half + i * 16, 16), 16)
            total = jnp.zeros((16, b), jnp.float32)
            for k in range(here):
                for t in range(terms):
                    total = total + weights[k * terms + t] * z_all[k, t, lines]
            acc[stage, d, lines] = total
            return carry

        lax.fori_loop(0, half // 16, step, 0)

    def share(stage, k, part):
        lines = pl.ds(part * half, half)
        return pltpu.make_async_remote_copy(
            src_ref=acc.at[stage, k, lines], dst_ref=got.at[stage, k, lines],
            send_sem=die_send.at[stage, k, part], recv_sem=die_recv.at[stage, k, part],
            device_id=other, device_id_type=MESH,
        )

    def far_middle(stage, k):
        for band in (0, 2):
            fill(stage, k, band, h, 0, b)
        far_rows(stage, k, 0)

    def own_sides(stage, k):
        for number in (3, 6):
            act(stage, k, number, "wait_recv")
        fill(stage, k, 1, 0, b, h)
        fill(stage, k, 1, h + b, b + h, h)
        own_rows(stage, k, b)

    def far_sides(stage, k):
        for number in (2, 4, 5, 7):
            act(stage, k, number, "wait_recv")
        for band in (0, 2):
            fill(stage, k, band, 0, b, h)
            fill(stage, k, band, h + b, b + h, h)
        far_rows(stage, k, b)

    def run_stage(stage):
        own_sides(stage, 0)
        for k in range(here):
            if k == 0:
                forward(stage, k)
            far_middle(stage, k)
            along(stage, k, 0)
            far_sides(stage, k)
            if k + 1 < here:
                own_sides(stage, k + 1)
                forward(stage, k + 1)
            along(stage, k, b)
        for k in range(here):
            for part in range(2):
                mix(stage, k, part)
                share(stage, k, part).start()
        for k in range(here):
            for part in range(2):
                mix(stage, here + k, part)

    label_all().wait_recv()
    for p in range(peers):
        label_rows[p : p + 1] = label_in[p]
    label_flat = label_rows[...].astype(jnp.bfloat16)
    lane_of = iota((128, slots), 1) % capacity
    held = iota((peers, slots), 1) // capacity == iota((peers, slots), 0)
    tile_line = (iota((tiles, slots), 0) + 1).astype(jnp.float32)
    tile_lane = (iota((slots, tiles), 1) + 1).astype(jnp.float32)
    eye_slots = iota((slots, slots), 0) == iota((slots, slots), 1)
    for k in range(here):
        pick = (iota((128, slots), 0) == lane_of + k * capacity).astype(jnp.bfloat16)
        label = jnp.sum(jnp.where(held, dot(label_flat, pick), 0.0), axis=0, keepdims=True)
        chosen_t = (tile_line == label).astype(jnp.bfloat16)
        label_col = jnp.sum(jnp.where(eye_slots, label, 0.0), axis=1, keepdims=True)
        chosen_keep[k] = (tile_lane == label_col).astype(jnp.bfloat16)
        swap_all(0, k).wait_recv()
        head, rest = two_halves(flat(arrived, k))
        totals = dot(
            jnp.concatenate([chosen_t, chosen_t], axis=1), jnp.concatenate([head, rest], axis=0)
        )
        field = exchange_blocks(totals)
        for part in range(2):
            begin_halo(0, k, field[part * half : (part + 1) * half], part)
        fill(0, k, 1, h, 0, b)
        own_rows(0, k, 0)
    run_stage(0)
    for k in range(here):
        for part in range(2):
            share(0, k, part).wait_recv()
            lines = slice(part * half, (part + 1) * half)
            heat = acc[0, here + k, lines] + got[0, k, lines]
            heat_ref[k, lines] = heat
            begin_halo(1, k, jax.nn.sigmoid(heat), part)
        fill(1, k, 1, h, 0, b)
        own_rows(1, k, 0)
    heat_done = pltpu.make_async_copy(heat_ref, heat_out, out_sems.at[here])
    heat_done.start()
    run_stage(1)
    for k in range(here):
        for part in range(2):
            share(1, k, part).wait_recv()
        patches = exchange_blocks(acc[1, here + k] + got[1, k])
        head, rest = two_halves(patches)
        chosen = chosen_keep[k]
        answer = dot(jnp.concatenate([chosen, chosen], axis=1), jnp.concatenate([head, rest], axis=0))
        for p in range(peers):
            answers[k, p] = answer[p * capacity : (p + 1) * capacity]
        start_each(functools.partial(swap_copy, 1, k))
        returned[k, me] = answers[k, me]
    for stage in range(2):
        for k in range(here):
            for number in range(10):
                act(stage, k, number, "wait_send")
            for part in range(2):
                share(stage, k, part).wait_send()
    label_all().wait_send()
    for k in range(here):
        swap_all(0, k).wait_send()
    for k in range(here):
        swap_all(1, k).wait_recv()
        head, rest = two_halves(flat(returned, k))
        place = place_keep[k]
        slopes_ref[k] = dot(
            jnp.concatenate([place, place], axis=1), jnp.concatenate([head, rest], axis=0)
        )
        pltpu.make_async_copy(slopes_ref.at[k], slopes_out.at[k], out_sems.at[k]).start()
    for k in range(here):
        swap_all(1, k).wait_send()
    heat_done.wait()
    for k in range(here):
        pltpu.make_async_copy(slopes_ref.at[k], slopes_out.at[k], out_sems.at[k]).wait()


def finish_kernel(heat_in, slopes_in, heat_out, slopes_out):
    heat_out[...] = heat_in[...]
    slopes_out[...] = slopes_in[...]


def finish(heat, slopes):
    vmem = pl.BlockSpec(memory_space=pltpu.VMEM)
    return pl.pallas_call(
        finish_kernel,
        out_shape=tuple(jax.ShapeDtypeStruct(x.shape, x.dtype) for x in (heat, slopes)),
        in_specs=[vmem, vmem],
        out_specs=(vmem, vmem),
    )(heat, slopes)


def local(parcel_patch, target_unit, target_patch, across_taps, down_taps, source_heated_mixing):
    here, blocks, cells = parcel_patch.shape
    terms, dies, _ = source_heated_mixing.shape
    peers = lax.axis_size(("row", "col"))
    capacity = max(2, 2 * blocks // peers)
    slots = peers * capacity
    a, b, h = UNIT_MESH_X, UNIT_MESH_Y, HALO
    w0, w1 = a + 2 * h, b + 2 * h
    anywhere = pl.BlockSpec(memory_space=pl.ANY)
    f32, bf16 = jnp.float32, jnp.bfloat16
    swap_buffer = pltpu.VMEM((here, peers, capacity, cells), f32)
    sems = pltpu.SemaphoreType.DMA
    heat, slopes = pl.pallas_call(
        kernel,
        out_shape=(
            jax.ShapeDtypeStruct((here, a, b), f32),
            jax.ShapeDtypeStruct((here, blocks, cells), f32),
        ),
        in_specs=[anywhere] * 5 + [pl.BlockSpec(memory_space=pltpu.SMEM)],
        out_specs=(anywhere, anywhere),
        scratch_shapes=[
            pltpu.VMEM(parcel_patch.shape, f32),
            pltpu.VMEM((here, blocks), jnp.int32),
            pltpu.VMEM((here, blocks), jnp.int32),
            pltpu.VMEM(across_taps.shape, f32),
            pltpu.VMEM(down_taps.shape, f32),
            pltpu.VMEM((here, a, b), f32),
            pltpu.VMEM((here, blocks, cells), f32),
            sems((5,)), sems((here + 1,)),
            swap_buffer, swap_buffer, swap_buffer, swap_buffer,
            pltpu.VMEM((peers, 1, 128), f32),
            pltpu.VMEM((peers, 1, 128), f32),
            pltpu.VMEM((peers, 128), f32),
            pltpu.VMEM((here, blocks, slots), bf16),
            pltpu.VMEM((here, slots, (a // PATCH_SIDE) * (b // PATCH_SIDE)), bf16),
            pltpu.VMEM((2, here, w0, w1), f32),
            pltpu.VMEM((2, terms * a, 3 * a), bf16),
            pltpu.VMEM((2, terms * a, 6 * h), bf16),
            pltpu.VMEM((2, terms, 2 * w1, b), bf16),
            pltpu.VMEM((here, 3 * a, w1), bf16),
            pltpu.VMEM((here, 6 * h, w1), bf16),
            pltpu.VMEM((here, terms * a, w1), f32),
            pltpu.VMEM((here, terms * a, 2 * w1), bf16),
            pltpu.VMEM((here, terms, a, b), f32),
            pltpu.VMEM((2, dies, a, b), f32),
            pltpu.VMEM((2, here, a, b), f32),
            sems((2, here)), sems((2, here)), sems((2,)),
            sems((2, here, 10)), sems((2, here, 10)),
            sems((2, here, 2)), sems((2, here, 2)),
        ],
        compiler_params=pltpu.CompilerParams(
            collective_id=0, has_side_effects=True, vmem_limit_bytes=56 * 2**20
        ),
    )(
        parcel_patch, target_unit.reshape(here, blocks), target_patch,
        across_taps, down_taps, source_heated_mixing.transpose(1, 2, 0),
    )
    return finish(heat, slopes)


def solution(mesh):
    placed = (
        P("die", ("row", "col"), None),
        P("die", ("row", "col"), None),
        P("die", ("row", "col")),
        P(),
        P(),
        P(),
    )
    return jax.shard_map(
        local,
        mesh=mesh,
        in_specs=placed,
        out_specs=(P("die", "row", "col"), P("die", ("row", "col"), None)),
        check_vma=False,
    )
```

```python
import functools

import jax
import jax.numpy as jnp
from jax import lax
from jax.experimental import pallas as pl
from jax.experimental.pallas import tpu as pltpu
from jax.sharding import PartitionSpec as P

PATCH_SIDE = 16
UNIT_MESH_X = 128
UNIT_MESH_Y = 256
HALO = 128
MESH = pl.DeviceIdType.MESH


def two_halves(values):
    head = values.astype(jnp.bfloat16)
    return head, (values - head.astype(jnp.float32)).astype(jnp.bfloat16)


def dot(left, right):
    return jnp.dot(left, right, preferred_element_type=jnp.float32)


def iota(shape, dim):
    return lax.broadcasted_iota(jnp.int32, shape, dim)


def exchange_blocks(x):
    rows = x.shape[0]
    left = x[:, :128].reshape(rows // 16, 2, 8, 128)
    right = x[:, 128:].reshape(rows // 16, 2, 8, 128)
    parts = [[left[:, 0], right[:, 0]], [left[:, 1], right[:, 1]]]
    parts[0][1], parts[1][0] = parts[1][0], parts[0][1]
    line, lane = iota((1, 8, 128), 1), iota((1, 8, 128), 2)

    def inner(v):
        for bit in range(3):
            d, w = 1 << bit, 16 << bit
            low_line, low_lane = (line & d) == 0, (lane & w) == 0
            first = pltpu.roll(pltpu.roll(v, 8 - d, 1), w, 2)
            second = first if bit == 2 else pltpu.roll(pltpu.roll(v, d, 1), 128 - w, 2)
            v = jnp.where(low_line == low_lane, v, jnp.where(low_line, first, second))
        return v

    columns = [
        jnp.stack([inner(parts[0][c]), inner(parts[1][c])], axis=1).reshape(rows, 128)
        for c in range(2)
    ]
    return jnp.concatenate(columns, axis=1)


def flat(parts):
    peers, capacity, cells = parts.shape
    if capacity % 8 == 0:
        return parts.reshape(peers * capacity, cells)
    return jnp.concatenate([parts[p] for p in range(peers)], axis=0)


def kernel(
    patch_in, unit_in, tile_in, across_in, down_in, mix_ref, heat_out, returned, place_out,
    patch_ref, unit_ref, tile_ref, across_ref, down_ref, heat_ref, in_sems, out_sems,
    outgoing, arrived, answers, label_out, label_in, label_rows,
    place_keep, chosen_keep, pads, a_own, a_halo, d_cat, p_own, p_halo, y_own, x_cat,
    z_all, acc, got, swap_send, swap_recv, label_sems, halo_send, halo_recv, die_send, die_recv,
):
    here, blocks, cells = patch_ref.shape
    terms = across_ref.shape[0]
    peers, capacity = outgoing.shape[1], outgoing.shape[2]
    slots = peers * capacity
    a, b, h = UNIT_MESH_X, UNIT_MESH_Y, HALO
    tiles = (a // PATCH_SIDE) * (b // PATCH_SIDE)
    row, col, die = lax.axis_index("row"), lax.axis_index("col"), lax.axis_index("die")
    rows_mesh, cols_mesh = lax.axis_size("row"), lax.axis_size("col")
    me = row * cols_mesh + col
    has_up, has_down = row > 0, row < rows_mesh - 1
    has_left, has_right = col > 0, col < cols_mesh - 1
    up, down, left, right = {"row": row - 1}, {"row": row + 1}, {"col": col - 1}, {"col": col + 1}
    other = {"die": 1 - die}

    def place_of(number):
        return {"row": number // cols_mesh, "col": number % cols_mesh}

    loads = [
        pltpu.make_async_copy(src, dst, in_sems.at[i])
        for i, (src, dst) in enumerate((
            (unit_in, unit_ref), (tile_in, tile_ref), (patch_in, patch_ref),
            (across_in, across_ref), (down_in, down_ref),
        ))
    ]
    for load in loads:
        load.start()
    barrier = pltpu.get_barrier_semaphore()

    def greet(i, carry):
        pl.semaphore_signal(barrier, inc=1, device_id=place_of((me + i) % peers), device_id_type=MESH)
        return carry

    lax.fori_loop(1, peers, greet, 0)
    pl.semaphore_signal(barrier, inc=1, device_id=other, device_id_type=MESH)

    for load in loads[:3]:
        load.wait()
    eye = iota((blocks, blocks), 0) == iota((blocks, blocks), 1)
    before = (iota((blocks, blocks), 1) < iota((blocks, blocks), 0)).astype(jnp.bfloat16)
    lanes = iota((blocks, 128), 1).astype(jnp.float32)
    slot_lane = iota((blocks, slots), 1).astype(jnp.float32)
    slot_line = iota((slots, blocks), 0).astype(jnp.float32)
    peer_line = iota((peers, blocks), 0).astype(jnp.float32)

    def column(line):
        return jnp.sum(jnp.where(eye, line, 0.0), axis=1, keepdims=True)

    def route(k):
        dest_row = unit_ref[k : k + 1, :].astype(jnp.float32)
        dest = column(dest_row)
        named = (dest == lanes).astype(jnp.bfloat16)
        count = dot(before, named)
        position = jnp.sum(named.astype(jnp.float32) * count, axis=1, keepdims=True)
        slot = dest * capacity + position
        slot_row = jnp.sum(jnp.where(eye, slot, 0.0), axis=0, keepdims=True)
        place_t = (slot_line == slot_row).astype(jnp.bfloat16)
        head, rest = two_halves(patch_ref[k])
        out = dot(
            jnp.concatenate([place_t, place_t], axis=1), jnp.concatenate([head, rest], axis=0)
        )
        for p in range(peers):
            outgoing[k, p] = out[p * capacity : (p + 1) * capacity]
        return dest_row, position, slot

    def label_part(k, dest_row, position):
        tile = column((tile_ref[k : k + 1, :] + 1).astype(jnp.float32))
        spread = jnp.where(lanes == position + k * capacity, tile, 0.0).astype(jnp.bfloat16)
        return dot((peer_line == dest_row).astype(jnp.bfloat16), spread)

    def swap_copy(stage, k, i):
        to = (me + i) % peers
        src, dst = (outgoing, arrived) if stage == 0 else (answers, returned)
        return pltpu.make_async_remote_copy(
            src_ref=src.at[k, to], dst_ref=dst.at[k, me],
            send_sem=swap_send.at[stage, k], recv_sem=swap_recv.at[stage, k],
            device_id=place_of(to), device_id_type=MESH,
        )

    def swap_all(stage, k):
        src, dst = (outgoing, arrived) if stage == 0 else (answers, returned)
        return pltpu.make_async_remote_copy(
            src_ref=src.at[k, pl.ds(0, peers - 1)], dst_ref=dst.at[k, pl.ds(0, peers - 1)],
            send_sem=swap_send.at[stage, k], recv_sem=swap_recv.at[stage, k],
            device_id=other, device_id_type=MESH,
        )

    def label_copy(i):
        to = (me + i) % peers
        return pltpu.make_async_remote_copy(
            src_ref=label_out.at[to], dst_ref=label_in.at[me],
            send_sem=label_sems.at[0], recv_sem=label_sems.at[1],
            device_id=place_of(to), device_id_type=MESH,
        )

    def label_all():
        return pltpu.make_async_remote_copy(
            src_ref=label_out.at[pl.ds(0, peers - 1)], dst_ref=label_in.at[pl.ds(0, peers - 1)],
            send_sem=label_sems.at[0], recv_sem=label_sems.at[1],
            device_id=other, device_id_type=MESH,
        )

    def start_each(make):
        def body(j, carry):
            make((j + peers // 2 - 2) % (peers - 1) + 1).start()
            return carry

        lax.fori_loop(1, peers, body, 0)

    routes = [route(0)]
    pl.semaphore_wait(barrier, peers)
    start_each(functools.partial(swap_copy, 0, 0))
    routes += [route(k) for k in range(1, here)]
    label_sum = sum(label_part(k, *routes[k][:2]) for k in range(here))
    for p in range(peers):
        label_out[p] = label_sum[p : p + 1]
    start_each(label_copy)
    for k in range(1, here):
        start_each(functools.partial(swap_copy, 0, k))
    label_in[me] = label_out[me]
    for k in range(here):
        place_keep[k] = (routes[k][2] == slot_lane).astype(jnp.bfloat16)
        arrived[k, me] = outgoing[k, me]
    place_done = pltpu.make_async_copy(place_keep, place_out, out_sems.at[0])
    place_done.start()

    w0, w1 = a + 2 * h, b + 2 * h
    for there, lines, cols in (
        (has_up, slice(0, h), slice(0, w1)),
        (has_down, slice(h + a, w0), slice(0, w1)),
        (has_left, slice(0, w0), slice(0, h)),
        (has_right, slice(0, w0), slice(h + b, w1)),
    ):
        @pl.when(jnp.logical_not(there))
        def _(lines=lines, cols=cols):
            part = pads[:, :, lines, cols]
            pads[:, :, lines, cols] = jnp.zeros_like(part)

    for load in loads[3:]:
        load.wait()
    u0, u1 = iota((across_ref.shape[1], 3 * h), 0), iota((across_ref.shape[1], 3 * h), 1)
    taps = across_ref.shape[1]

    def base(taps_ref, flipped):
        pick = (u1 == (taps - u0 if flipped else u0 + 1)).astype(jnp.float32)
        return jnp.dot(
            taps_ref[...], pick, precision=lax.Precision.HIGHEST, preferred_element_type=jnp.float32
        )

    none = jnp.zeros((h, h), jnp.bfloat16)
    for stage in range(2):
        across_base = base(across_ref, stage == 1)
        down_base = base(down_ref, stage == 0)
        for t in range(terms):
            lines = pl.ds(t * a, a)
            span = jnp.broadcast_to(across_base[t : t + 1, :], (a, 3 * h))
            head, rest = two_halves(pltpu.roll(span, 0, 1, stride=1, stride_axis=0))
            for part, piece in enumerate((head, head, rest)):
                a_own[stage, lines, part * a : (part + 1) * a] = piece[:, h : 2 * h]
                a_halo[stage, lines, part * 2 * h : part * 2 * h + h] = piece[:, :h]
                a_halo[stage, lines, part * 2 * h + h : (part + 1) * 2 * h] = piece[:, 2 * h :]
            wide = jnp.broadcast_to(down_base[t : t + 1, :], (3 * h, 3 * h))
            wide = pltpu.roll(wide, h, 1, stride=1, stride_axis=0)[:, :h]
            w = b + 2 * h
            for part, piece in enumerate(two_halves(wide)):
                at = part * w
                d_cat[stage, t, at : at + b, 0:h] = piece[h : 3 * h]
                d_cat[stage, t, at : at + b, h:b] = piece[0:b]
                d_cat[stage, t, at + b : at + b + h, 0:h] = piece[0:h]
                d_cat[stage, t, at + b : at + b + h, h:b] = none
                d_cat[stage, t, at + b + h : at + w, 0:h] = none
                d_cat[stage, t, at + b + h : at + w, h:b] = piece[2 * h :]

    tops, sizes, half = (0, h, h + a), (h, a, h), a // 2

    def halo(stage, which, number, part=None):
        def block(band, start, width):
            lines = pl.ds(tops[band], sizes[band]) if part is None else pl.ds(tops[band] + part * half, half)
            return pads.at[stage, which, lines, pl.ds(start, width)]

        if number == 0:
            src, dst, device = block(1, h, b), block(2, h, b), up
        elif number == 1:
            src, dst, device = block(1, h, b), block(0, h, b), down
        elif number < 5:
            src, dst, device = block(number - 2, h, h), block(number - 2, h + b, h), left
        else:
            src, dst, device = block(number - 5, b, h), block(number - 5, 0, h), right
        arrival = halo_recv.at[stage, which if isinstance(which, int) else 0, number]
        return pltpu.make_async_remote_copy(
            src_ref=src, dst_ref=dst, send_sem=halo_send.at[stage, number], recv_sem=arrival,
            device_id=device, device_id_type=MESH,
        )

    rows_of = (has_up, None, has_down)

    def both(x, y):
        return y if x is None else jnp.logical_and(x, y)

    sends = [has_up, has_down] + [both(r, has_left) for r in rows_of] + [both(r, has_right) for r in rows_of]
    gets = [has_down, has_up] + [both(r, has_right) for r in rows_of] + [both(r, has_left) for r in rows_of]

    def act(stage, which, number, what, part=None):
        @pl.when(gets[number] if what == "wait_recv" else sends[number])
        def _():
            getattr(halo(stage, which, number, part), what)()

    def begin_halo(stage, k, field, part):
        pads[stage, k, h + part * half : h + (part + 1) * half, h : h + b] = field
        for number in (0, 1):
            act(stage, k, number, "start", part)
        if part == 1:
            for number in (3, 6):
                act(stage, k, number, "start")

    def forward(stage, k):
        for from_down, corners in ((0, (4, 7)), (1, (2, 5))):
            act(stage, k, from_down, "wait_recv")
            for number in corners:
                act(stage, k, number, "start")

    def fill(stage, k, band, source, at, width):
        head, rest = two_halves(pads[stage, k, tops[band] : tops[band] + sizes[band], source : source + width])
        cols = slice(at, at + width)
        if band == 1:
            for part, piece in enumerate((head, rest, head)):
                p_own[k, part * a : (part + 1) * a, cols] = piece
        else:
            off = 0 if band == 0 else h
            for part, piece in enumerate((head, rest, head)):
                p_halo[k, part * 2 * h + off : part * 2 * h + off + h, cols] = piece

    def own_rows(stage, k, at):
        cols = slice(at, at + b)
        y_own[k, :, cols] = dot(a_own[stage], p_own[k, :, cols])

    def far_rows(stage, k, at):
        cols = slice(at, at + b)
        total = dot(a_halo[stage], p_halo[k, :, cols]) + y_own[k, :, cols]
        head, rest = two_halves(total)
        x_cat[k, :, cols] = head
        x_cat[k, :, at + b + 2 * h : at + 2 * b + 2 * h] = rest

    def along(stage, k, at):
        w = b + 2 * h
        head_cols, rest_cols = slice(at, at + b), slice(w + at, w + at + b)

        def step(t, carry):
            lines = pl.ds(pl.multiple_of(t * a, a), a)
            head, rest = x_cat[k, lines, head_cols], x_cat[k, lines, rest_cols]
            d_head, d_rest = d_cat[stage, t, head_cols], d_cat[stage, t, rest_cols]
            z = dot(
                jnp.concatenate([head, head, rest], axis=1),
                jnp.concatenate([d_head, d_rest, d_head], axis=0),
            )
            z_all[k, t] = z if at == 0 else z_all[k, t] + z
            return carry

        lax.fori_loop(0, terms, step, 0, unroll=True)

    def mix(stage, d, part):
        target = ((1 - die) if d < here else die) * here + d % here
        weights = []
        for k in range(here):
            source = die * here + k
            for t in range(terms):
                pair = (target, source) if stage == 0 else (source, target)
                weights.append(mix_ref[pair[0], pair[1], t])

        def step(i, carry):
            lines = pl.ds(pl.multiple_of(part * half + i * 16, 16), 16)
            total = jnp.zeros((16, b), jnp.float32)
            for k in range(here):
                for t in range(terms):
                    total = total + weights[k * terms + t] * z_all[k, t, lines]
            acc[stage, d, lines] = total
            return carry

        lax.fori_loop(0, half // 16, step, 0)

    def share(stage, k, part):
        lines = pl.ds(part * half, half)
        return pltpu.make_async_remote_copy(
            src_ref=acc.at[stage, k, lines], dst_ref=got.at[stage, k, lines],
            send_sem=die_send.at[stage, k, part], recv_sem=die_recv.at[stage, k, part],
            device_id=other, device_id_type=MESH,
        )

    def far_middle(stage, k):
        for band in (0, 2):
            fill(stage, k, band, h, 0, b)
        far_rows(stage, k, 0)

    def own_sides(stage, k):
        for number in (3, 6):
            act(stage, k, number, "wait_recv")
        fill(stage, k, 1, 0, b, h)
        fill(stage, k, 1, h + b, b + h, h)
        own_rows(stage, k, b)

    def far_sides(stage, k):
        for number in (2, 4, 5, 7):
            act(stage, k, number, "wait_recv")
        for band in (0, 2):
            fill(stage, k, band, 0, b, h)
            fill(stage, k, band, h + b, b + h, h)
        far_rows(stage, k, b)

    def run_stage(stage):
        own_sides(stage, 0)
        for k in range(here):
            if k == 0:
                forward(stage, k)
            far_middle(stage, k)
            along(stage, k, 0)
            far_sides(stage, k)
            if k + 1 < here:
                own_sides(stage, k + 1)
                forward(stage, k + 1)
            along(stage, k, b)
        for k in range(here):
            for part in range(2):
                mix(stage, k, part)
                share(stage, k, part).start()
        for k in range(here):
            for part in range(2):
                mix(stage, here + k, part)

    label_all().wait_recv()
    for p in range(peers):
        label_rows[p : p + 1] = label_in[p]
    label_flat = label_rows[...].astype(jnp.bfloat16)
    lane_of = iota((128, slots), 1) % capacity
    held = iota((peers, slots), 1) // capacity == iota((peers, slots), 0)
    tile_line = (iota((tiles, slots), 0) + 1).astype(jnp.float32)
    tile_lane = (iota((slots, tiles), 1) + 1).astype(jnp.float32)
    eye_slots = iota((slots, slots), 0) == iota((slots, slots), 1)
    for k in range(here):
        pick = (iota((128, slots), 0) == lane_of + k * capacity).astype(jnp.bfloat16)
        label = jnp.sum(jnp.where(held, dot(label_flat, pick), 0.0), axis=0, keepdims=True)
        chosen_t = (tile_line == label).astype(jnp.bfloat16)
        label_col = jnp.sum(jnp.where(eye_slots, label, 0.0), axis=1, keepdims=True)
        chosen_keep[k] = (tile_lane == label_col).astype(jnp.bfloat16)
        swap_all(0, k).wait_recv()
        head, rest = two_halves(flat(arrived[k]))
        totals = dot(
            jnp.concatenate([chosen_t, chosen_t], axis=1), jnp.concatenate([head, rest], axis=0)
        )
        field = exchange_blocks(totals)
        for part in range(2):
            begin_halo(0, k, field[part * half : (part + 1) * half], part)
        fill(0, k, 1, h, 0, b)
        own_rows(0, k, 0)
    run_stage(0)
    for k in range(here):
        for part in range(2):
            share(0, k, part).wait_recv()
            lines = slice(part * half, (part + 1) * half)
            heat = acc[0, here + k, lines] + got[0, k, lines]
            heat_ref[k, lines] = heat
            begin_halo(1, k, jax.nn.sigmoid(heat), part)
        fill(1, k, 1, h, 0, b)
        own_rows(1, k, 0)
    def stay(k):
        return pltpu.make_async_copy(answers.at[k, me], returned.at[k, me], out_sems.at[2 + k])

    heat_done = pltpu.make_async_copy(heat_ref, heat_out, out_sems.at[1])
    heat_done.start()
    run_stage(1)
    for k in range(here):
        for part in range(2):
            share(1, k, part).wait_recv()
        patches = exchange_blocks(acc[1, here + k] + got[1, k])
        head, rest = two_halves(patches)
        chosen = chosen_keep[k]
        answer = dot(jnp.concatenate([chosen, chosen], axis=1), jnp.concatenate([head, rest], axis=0))
        for p in range(peers):
            answers[k, p] = answer[p * capacity : (p + 1) * capacity]
        start_each(functools.partial(swap_copy, 1, k))
        stay(k).start()
    for stage in range(2):
        for number in range(8):
            act(stage, pl.ds(0, here), number, "wait_send")
        for k in range(here):
            for part in range(2):
                share(stage, k, part).wait_send()
    label_all().wait_send()
    for k in range(here):
        swap_all(0, k).wait_send()
    place_done.wait()
    heat_done.wait()
    for k in range(here):
        stay(k).wait()
        swap_all(1, k).wait_recv()
    for k in range(here):
        swap_all(1, k).wait_send()


def finish_kernel(heat_in, returned, place_in, heat_out, slopes_out):
    heat_out[...] = heat_in[...]
    for k in range(place_in.shape[0]):
        head, rest = two_halves(flat(returned[k]))
        place = place_in[k]
        slopes_out[k] = dot(
            jnp.concatenate([place, place], axis=1), jnp.concatenate([head, rest], axis=0)
        )


def finish(heat, returned, place):
    here, peers, capacity, cells = returned.shape
    blocks, slots = place.shape[1:]
    outs = (heat.shape, (here, blocks, cells))

    def spec(shape):
        return pl.BlockSpec((1, *shape[1:]), lambda k: (k,) + (0,) * (len(shape) - 1))

    return pl.pallas_call(
        finish_kernel,
        grid=(here,),
        out_shape=tuple(jax.ShapeDtypeStruct(x, jnp.float32) for x in outs),
        in_specs=[spec(heat.shape), spec(returned.shape), spec(place.shape)],
        out_specs=tuple(spec(x) for x in outs),
    )(heat, returned, place)


def local(parcel_patch, target_unit, target_patch, across_taps, down_taps, source_heated_mixing):
    here, blocks, cells = parcel_patch.shape
    terms, dies, _ = source_heated_mixing.shape
    peers = lax.axis_size(("row", "col"))
    capacity = max(2, 2 * blocks // peers)
    slots = peers * capacity
    a, b, h = UNIT_MESH_X, UNIT_MESH_Y, HALO
    w0, w1 = a + 2 * h, b + 2 * h
    anywhere = pl.BlockSpec(memory_space=pl.ANY)
    f32, bf16 = jnp.float32, jnp.bfloat16
    swap_buffer = pltpu.VMEM((here, peers, capacity, cells), f32)
    sems = pltpu.SemaphoreType.DMA
    heat, returned, place = pl.pallas_call(
        kernel,
        out_shape=(
            jax.ShapeDtypeStruct((here, a, b), f32),
            jax.ShapeDtypeStruct((here, peers, capacity, cells), f32),
            jax.ShapeDtypeStruct((here, blocks, slots), bf16),
        ),
        in_specs=[anywhere] * 5 + [pl.BlockSpec(memory_space=pltpu.SMEM)],
        out_specs=(anywhere,) * 3,
        scratch_shapes=[
            pltpu.VMEM(parcel_patch.shape, f32),
            pltpu.VMEM((here, blocks), jnp.int32),
            pltpu.VMEM((here, blocks), jnp.int32),
            pltpu.VMEM(across_taps.shape, f32),
            pltpu.VMEM(down_taps.shape, f32),
            pltpu.VMEM((here, a, b), f32),
            sems((5,)), sems((here + 2,)),
            swap_buffer, swap_buffer, swap_buffer,
            pltpu.VMEM((peers, 1, 128), f32),
            pltpu.VMEM((peers, 1, 128), f32),
            pltpu.VMEM((peers, 128), f32),
            pltpu.VMEM((here, blocks, slots), bf16),
            pltpu.VMEM((here, slots, (a // PATCH_SIDE) * (b // PATCH_SIDE)), bf16),
            pltpu.VMEM((2, here, w0, w1), f32),
            pltpu.VMEM((2, terms * a, 3 * a), bf16),
            pltpu.VMEM((2, terms * a, 6 * h), bf16),
            pltpu.VMEM((2, terms, 2 * w1, b), bf16),
            pltpu.VMEM((here, 3 * a, w1), bf16),
            pltpu.VMEM((here, 6 * h, w1), bf16),
            pltpu.VMEM((here, terms * a, w1), f32),
            pltpu.VMEM((here, terms * a, 2 * w1), bf16),
            pltpu.VMEM((here, terms, a, b), f32),
            pltpu.VMEM((2, dies, a, b), f32),
            pltpu.VMEM((2, here, a, b), f32),
            sems((2, here)), sems((2, here)), sems((2,)),
            sems((2, 8)), sems((2, here, 8)),
            sems((2, here, 2)), sems((2, here, 2)),
        ],
        compiler_params=pltpu.CompilerParams(
            collective_id=0, has_side_effects=True, vmem_limit_bytes=56 * 2**20
        ),
    )(
        parcel_patch, target_unit.reshape(here, blocks), target_patch,
        across_taps, down_taps, source_heated_mixing.transpose(1, 2, 0),
    )
    return finish(heat, returned, place)


def solution(mesh):
    placed = (
        P("die", ("row", "col"), None),
        P("die", ("row", "col"), None),
        P("die", ("row", "col")),
        P(),
        P(),
        P(),
    )
    return jax.shard_map(
        local,
        mesh=mesh,
        in_specs=placed,
        out_specs=(P("die", "row", "col"), P("die", ("row", "col"), None)),
        check_vma=False,
    )
```

```python
import functools

import jax
import jax.numpy as jnp
from jax import lax
from jax.experimental import pallas as pl
from jax.experimental.pallas import tpu as pltpu
from jax.sharding import PartitionSpec as P

PATCH_SIDE = 16
UNIT_MESH_X = 128
UNIT_MESH_Y = 256
HALO = 128
MESH = pl.DeviceIdType.MESH


def two_halves(values):
    head = values.astype(jnp.bfloat16)
    return head, (values - head.astype(jnp.float32)).astype(jnp.bfloat16)


def dot(left, right):
    return jnp.dot(left, right, preferred_element_type=jnp.float32)


def iota(shape, dim):
    return lax.broadcasted_iota(jnp.int32, shape, dim)


def exchange_blocks(x):
    rows = x.shape[0]
    left = x[:, :128].reshape(rows // 16, 2, 8, 128)
    right = x[:, 128:].reshape(rows // 16, 2, 8, 128)
    parts = [[left[:, 0], right[:, 0]], [left[:, 1], right[:, 1]]]
    parts[0][1], parts[1][0] = parts[1][0], parts[0][1]
    line, lane = iota((1, 8, 128), 1), iota((1, 8, 128), 2)

    def inner(v):
        for bit in range(3):
            d, w = 1 << bit, 16 << bit
            low_line, low_lane = (line & d) == 0, (lane & w) == 0
            first = pltpu.roll(pltpu.roll(v, 8 - d, 1), w, 2)
            second = first if bit == 2 else pltpu.roll(pltpu.roll(v, d, 1), 128 - w, 2)
            v = jnp.where(low_line == low_lane, v, jnp.where(low_line, first, second))
        return v

    columns = [
        jnp.stack([inner(parts[0][c]), inner(parts[1][c])], axis=1).reshape(rows, 128)
        for c in range(2)
    ]
    return jnp.concatenate(columns, axis=1)


def flat(parts):
    peers, capacity, cells = parts.shape
    if capacity % 8 == 0:
        return parts.reshape(peers * capacity, cells)
    return jnp.concatenate([parts[p] for p in range(peers)], axis=0)


def kernel(
    patch_in, unit_in, tile_in, across_in, down_in, mix_ref, heat_out, returned, place_out,
    patch_ref, unit_ref, tile_ref, across_ref, down_ref, heat_ref, in_sems, out_sems,
    outgoing, arrived, answers, label_out, label_in, label_rows,
    place_keep, chosen_keep, pads, a_own, a_halo, d_cat, p_own, p_halo, y_own, x_cat,
    z_all, acc, got, swap_send, swap_recv, label_sems, halo_send, halo_recv, die_send, die_recv,
):
    here, blocks, cells = patch_ref.shape
    terms = across_ref.shape[0]
    peers, capacity = outgoing.shape[1], outgoing.shape[2]
    slots = peers * capacity
    a, b, h = UNIT_MESH_X, UNIT_MESH_Y, HALO
    tiles = (a // PATCH_SIDE) * (b // PATCH_SIDE)
    row, col, die = lax.axis_index("row"), lax.axis_index("col"), lax.axis_index("die")
    rows_mesh, cols_mesh = lax.axis_size("row"), lax.axis_size("col")
    me = row * cols_mesh + col
    has_up, has_down = row > 0, row < rows_mesh - 1
    has_left, has_right = col > 0, col < cols_mesh - 1
    up, down, left, right = {"row": row - 1}, {"row": row + 1}, {"col": col - 1}, {"col": col + 1}
    other = {"die": 1 - die}

    def place_of(number):
        return {"row": number // cols_mesh, "col": number % cols_mesh}

    loads = [
        pltpu.make_async_copy(src, dst, in_sems.at[i])
        for i, (src, dst) in enumerate((
            (unit_in, unit_ref), (tile_in, tile_ref), (patch_in, patch_ref),
            (across_in, across_ref), (down_in, down_ref),
        ))
    ]
    for load in loads:
        load.start()
    barrier = pltpu.get_barrier_semaphore()

    def greet(i, carry):
        pl.semaphore_signal(barrier, inc=1, device_id=place_of((me + i) % peers), device_id_type=MESH)
        return carry

    lax.fori_loop(1, peers, greet, 0)
    pl.semaphore_signal(barrier, inc=1, device_id=other, device_id_type=MESH)

    for load in loads[:3]:
        load.wait()
    eye = iota((blocks, blocks), 0) == iota((blocks, blocks), 1)
    before = (iota((blocks, blocks), 1) < iota((blocks, blocks), 0)).astype(jnp.bfloat16)
    lanes = iota((blocks, 128), 1).astype(jnp.float32)
    slot_lane = iota((blocks, slots), 1).astype(jnp.float32)
    slot_line = iota((slots, blocks), 0).astype(jnp.float32)
    peer_line = iota((peers, blocks), 0).astype(jnp.float32)

    def column(line):
        return jnp.sum(jnp.where(eye, line, 0.0), axis=1, keepdims=True)

    def route(k):
        dest_row = unit_ref[k : k + 1, :].astype(jnp.float32)
        dest = column(dest_row)
        named = (dest == lanes).astype(jnp.bfloat16)
        count = dot(before, named)
        position = jnp.sum(named.astype(jnp.float32) * count, axis=1, keepdims=True)
        slot = dest * capacity + position
        slot_row = jnp.sum(jnp.where(eye, slot, 0.0), axis=0, keepdims=True)
        place_t = (slot_line == slot_row).astype(jnp.bfloat16)
        head, rest = two_halves(patch_ref[k])
        out = dot(
            jnp.concatenate([place_t, place_t], axis=1), jnp.concatenate([head, rest], axis=0)
        )
        for p in range(peers):
            outgoing[k, p] = out[p * capacity : (p + 1) * capacity]
        return dest_row, position, slot

    def label_part(k, dest_row, position):
        tile = column((tile_ref[k : k + 1, :] + 1).astype(jnp.float32))
        spread = jnp.where(lanes == position + k * capacity, tile, 0.0).astype(jnp.bfloat16)
        return dot((peer_line == dest_row).astype(jnp.bfloat16), spread)

    def swap_copy(stage, k, i):
        to = (me + i) % peers
        src, dst = (outgoing, arrived) if stage == 0 else (answers, returned)
        return pltpu.make_async_remote_copy(
            src_ref=src.at[k, to], dst_ref=dst.at[k, me],
            send_sem=swap_send.at[stage, k], recv_sem=swap_recv.at[stage, k],
            device_id=place_of(to), device_id_type=MESH,
        )

    def swap_all(stage, k):
        src, dst = (outgoing, arrived) if stage == 0 else (answers, returned)
        return pltpu.make_async_remote_copy(
            src_ref=src.at[k, pl.ds(0, peers - 1)], dst_ref=dst.at[k, pl.ds(0, peers - 1)],
            send_sem=swap_send.at[stage, k], recv_sem=swap_recv.at[stage, k],
            device_id=other, device_id_type=MESH,
        )

    def label_copy(i):
        to = (me + i) % peers
        return pltpu.make_async_remote_copy(
            src_ref=label_out.at[to], dst_ref=label_in.at[me],
            send_sem=label_sems.at[0], recv_sem=label_sems.at[1],
            device_id=place_of(to), device_id_type=MESH,
        )

    def label_all():
        return pltpu.make_async_remote_copy(
            src_ref=label_out.at[pl.ds(0, peers - 1)], dst_ref=label_in.at[pl.ds(0, peers - 1)],
            send_sem=label_sems.at[0], recv_sem=label_sems.at[1],
            device_id=other, device_id_type=MESH,
        )

    def start_each(make):
        def body(j, carry):
            make(j).start()
            return carry

        lax.fori_loop(1, peers, body, 0)

    routes = [route(0)]
    pl.semaphore_wait(barrier, peers)
    start_each(functools.partial(swap_copy, 0, 0))
    routes += [route(k) for k in range(1, here)]
    label_sum = sum(label_part(k, *routes[k][:2]) for k in range(here))
    for p in range(peers):
        label_out[p] = label_sum[p : p + 1]
    start_each(label_copy)
    for k in range(1, here):
        start_each(functools.partial(swap_copy, 0, k))
    label_in[me] = label_out[me]
    for k in range(here):
        place_keep[k] = (routes[k][2] == slot_lane).astype(jnp.bfloat16)
        arrived[k, me] = outgoing[k, me]
    place_done = pltpu.make_async_copy(place_keep, place_out, out_sems.at[0])
    place_done.start()

    w0, w1 = a + 2 * h, b + 2 * h
    for there, lines, cols in (
        (has_up, slice(0, h), slice(0, w1)),
        (has_down, slice(h + a, w0), slice(0, w1)),
        (has_left, slice(0, w0), slice(0, h)),
        (has_right, slice(0, w0), slice(h + b, w1)),
    ):
        @pl.when(jnp.logical_not(there))
        def _(lines=lines, cols=cols):
            part = pads[:, :, lines, cols]
            pads[:, :, lines, cols] = jnp.zeros_like(part)

    for load in loads[3:]:
        load.wait()
    u0, u1 = iota((across_ref.shape[1], 3 * h), 0), iota((across_ref.shape[1], 3 * h), 1)
    taps = across_ref.shape[1]

    def base(taps_ref, flipped):
        pick = (u1 == (taps - u0 if flipped else u0 + 1)).astype(jnp.float32)
        return jnp.dot(
            taps_ref[...], pick, precision=lax.Precision.HIGHEST, preferred_element_type=jnp.float32
        )

    none = jnp.zeros((h, h), jnp.bfloat16)
    for stage in range(2):
        across_base = base(across_ref, stage == 1)
        down_base = base(down_ref, stage == 0)
        for t in range(terms):
            lines = pl.ds(t * a, a)
            span = jnp.broadcast_to(across_base[t : t + 1, :], (a, 3 * h))
            head, rest = two_halves(pltpu.roll(span, 0, 1, stride=1, stride_axis=0))
            for part, piece in enumerate((head, head, rest)):
                a_own[stage, lines, part * a : (part + 1) * a] = piece[:, h : 2 * h]
                a_halo[stage, lines, part * 2 * h : part * 2 * h + h] = piece[:, :h]
                a_halo[stage, lines, part * 2 * h + h : (part + 1) * 2 * h] = piece[:, 2 * h :]
            wide = jnp.broadcast_to(down_base[t : t + 1, :], (3 * h, 3 * h))
            wide = pltpu.roll(wide, h, 1, stride=1, stride_axis=0)[:, :h]
            w = b + 2 * h
            for part, piece in enumerate(two_halves(wide)):
                at = part * w
                d_cat[stage, t, at : at + b, 0:h] = piece[h : 3 * h]
                d_cat[stage, t, at : at + b, h:b] = piece[0:b]
                d_cat[stage, t, at + b : at + b + h, 0:h] = piece[0:h]
                d_cat[stage, t, at + b : at + b + h, h:b] = none
                d_cat[stage, t, at + b + h : at + w, 0:h] = none
                d_cat[stage, t, at + b + h : at + w, h:b] = piece[2 * h :]

    tops, sizes, half = (0, h, h + a), (h, a, h), a // 2

    def halo(stage, which, number, part=None):
        def block(band, start, width):
            lines = pl.ds(tops[band], sizes[band]) if part is None else pl.ds(tops[band] + part * half, half)
            return pads.at[stage, which, lines, pl.ds(start, width)]

        if number == 0:
            src, dst, device = block(1, h, b), block(2, h, b), up
        elif number == 1:
            src, dst, device = block(1, h, b), block(0, h, b), down
        elif number < 5:
            src, dst, device = block(number - 2, h, h), block(number - 2, h + b, h), left
        else:
            src, dst, device = block(number - 5, b, h), block(number - 5, 0, h), right
        arrival = halo_recv.at[stage, which if isinstance(which, int) else 0, number]
        return pltpu.make_async_remote_copy(
            src_ref=src, dst_ref=dst, send_sem=halo_send.at[stage, number], recv_sem=arrival,
            device_id=device, device_id_type=MESH,
        )

    rows_of = (has_up, None, has_down)

    def both(x, y):
        return y if x is None else jnp.logical_and(x, y)

    sends = [has_up, has_down] + [both(r, has_left) for r in rows_of] + [both(r, has_right) for r in rows_of]
    gets = [has_down, has_up] + [both(r, has_right) for r in rows_of] + [both(r, has_left) for r in rows_of]

    def act(stage, which, number, what, part=None):
        @pl.when(gets[number] if what == "wait_recv" else sends[number])
        def _():
            getattr(halo(stage, which, number, part), what)()

    def begin_halo(stage, k, field, part):
        pads[stage, k, h + part * half : h + (part + 1) * half, h : h + b] = field
        for number in (0, 1):
            act(stage, k, number, "start", part)
        if part == 1:
            for number in (3, 6):
                act(stage, k, number, "start")

    def forward(stage, k):
        for from_down, corners in ((0, (4, 7)), (1, (2, 5))):
            act(stage, k, from_down, "wait_recv")
            for number in corners:
                act(stage, k, number, "start")

    def fill(stage, k, band, source, at, width):
        head, rest = two_halves(pads[stage, k, tops[band] : tops[band] + sizes[band], source : source + width])
        cols = slice(at, at + width)
        if band == 1:
            for part, piece in enumerate((head, rest, head)):
                p_own[k, part * a : (part + 1) * a, cols] = piece
        else:
            off = 0 if band == 0 else h
            for part, piece in enumerate((head, rest, head)):
                p_halo[k, part * 2 * h + off : part * 2 * h + off + h, cols] = piece

    def own_rows(stage, k, at):
        cols = slice(at, at + b)
        y_own[k, :, cols] = dot(a_own[stage], p_own[k, :, cols])

    def far_rows(stage, k, at):
        cols = slice(at, at + b)
        total = dot(a_halo[stage], p_halo[k, :, cols]) + y_own[k, :, cols]
        head, rest = two_halves(total)
        x_cat[k, :, cols] = head
        x_cat[k, :, at + b + 2 * h : at + 2 * b + 2 * h] = rest

    def along(stage, k, at):
        w = b + 2 * h
        head_cols, rest_cols = slice(at, at + b), slice(w + at, w + at + b)

        def step(t, carry):
            lines = pl.ds(pl.multiple_of(t * a, a), a)
            head, rest = x_cat[k, lines, head_cols], x_cat[k, lines, rest_cols]
            d_head, d_rest = d_cat[stage, t, head_cols], d_cat[stage, t, rest_cols]
            z = dot(
                jnp.concatenate([head, head, rest], axis=1),
                jnp.concatenate([d_head, d_rest, d_head], axis=0),
            )
            z_all[k, t] = z if at == 0 else z_all[k, t] + z
            return carry

        lax.fori_loop(0, terms, step, 0, unroll=True)

    def mix(stage, d, part):
        target = ((1 - die) if d < here else die) * here + d % here
        weights = []
        for k in range(here):
            source = die * here + k
            for t in range(terms):
                pair = (target, source) if stage == 0 else (source, target)
                weights.append(mix_ref[pair[0], pair[1], t])

        def step(i, carry):
            lines = pl.ds(pl.multiple_of(part * half + i * 16, 16), 16)
            total = jnp.zeros((16, b), jnp.float32)
            for k in range(here):
                for t in range(terms):
                    total = total + weights[k * terms + t] * z_all[k, t, lines]
            acc[stage, d, lines] = total
            return carry

        lax.fori_loop(0, half // 16, step, 0)

    def share(stage, k, part):
        lines = pl.ds(part * half, half)
        return pltpu.make_async_remote_copy(
            src_ref=acc.at[stage, k, lines], dst_ref=got.at[stage, k, lines],
            send_sem=die_send.at[stage, k, part], recv_sem=die_recv.at[stage, k, part],
            device_id=other, device_id_type=MESH,
        )

    def far_middle(stage, k):
        for band in (0, 2):
            fill(stage, k, band, h, 0, b)
        far_rows(stage, k, 0)

    def own_sides(stage, k):
        for number in (3, 6):
            act(stage, k, number, "wait_recv")
        fill(stage, k, 1, 0, b, h)
        fill(stage, k, 1, h + b, b + h, h)
        own_rows(stage, k, b)

    def far_sides(stage, k):
        for number in (2, 4, 5, 7):
            act(stage, k, number, "wait_recv")
        for band in (0, 2):
            fill(stage, k, band, 0, b, h)
            fill(stage, k, band, h + b, b + h, h)
        far_rows(stage, k, b)

    def run_stage(stage):
        own_sides(stage, 0)
        for k in range(here):
            if k == 0:
                forward(stage, k)
            far_middle(stage, k)
            along(stage, k, 0)
            far_sides(stage, k)
            if k + 1 < here:
                own_sides(stage, k + 1)
                forward(stage, k + 1)
            along(stage, k, b)
        for k in range(here):
            for part in range(2):
                mix(stage, k, part)
                share(stage, k, part).start()
        for k in range(here):
            for part in range(2):
                mix(stage, here + k, part)

    label_all().wait_recv()
    for p in range(peers):
        label_rows[p : p + 1] = label_in[p]
    label_flat = label_rows[...].astype(jnp.bfloat16)
    lane_of = iota((128, slots), 1) % capacity
    held = iota((peers, slots), 1) // capacity == iota((peers, slots), 0)
    tile_line = (iota((tiles, slots), 0) + 1).astype(jnp.float32)
    tile_lane = (iota((slots, tiles), 1) + 1).astype(jnp.float32)
    eye_slots = iota((slots, slots), 0) == iota((slots, slots), 1)
    for k in range(here):
        pick = (iota((128, slots), 0) == lane_of + k * capacity).astype(jnp.bfloat16)
        label = jnp.sum(jnp.where(held, dot(label_flat, pick), 0.0), axis=0, keepdims=True)
        chosen_t = (tile_line == label).astype(jnp.bfloat16)
        label_col = jnp.sum(jnp.where(eye_slots, label, 0.0), axis=1, keepdims=True)
        chosen_keep[k] = (tile_lane == label_col).astype(jnp.bfloat16)
        swap_all(0, k).wait_recv()
        head, rest = two_halves(flat(arrived[k]))
        totals = dot(
            jnp.concatenate([chosen_t, chosen_t], axis=1), jnp.concatenate([head, rest], axis=0)
        )
        field = exchange_blocks(totals)
        for part in range(2):
            begin_halo(0, k, field[part * half : (part + 1) * half], part)
        fill(0, k, 1, h, 0, b)
        own_rows(0, k, 0)
    run_stage(0)
    for k in range(here):
        for part in range(2):
            share(0, k, part).wait_recv()
            lines = slice(part * half, (part + 1) * half)
            heat = acc[0, here + k, lines] + got[0, k, lines]
            heat_ref[k, lines] = heat
            begin_halo(1, k, jax.nn.sigmoid(heat), part)
        fill(1, k, 1, h, 0, b)
        own_rows(1, k, 0)
    def stay(k):
        return pltpu.make_async_copy(answers.at[k, me], returned.at[k, me], out_sems.at[2 + k])

    heat_done = pltpu.make_async_copy(heat_ref, heat_out, out_sems.at[1])
    heat_done.start()
    run_stage(1)
    for k in range(here):
        for part in range(2):
            share(1, k, part).wait_recv()
        patches = exchange_blocks(acc[1, here + k] + got[1, k])
        head, rest = two_halves(patches)
        chosen = chosen_keep[k]
        answer = dot(jnp.concatenate([chosen, chosen], axis=1), jnp.concatenate([head, rest], axis=0))
        for p in range(peers):
            answers[k, p] = answer[p * capacity : (p + 1) * capacity]
        start_each(functools.partial(swap_copy, 1, k))
        stay(k).start()
    for stage in range(2):
        for number in range(8):
            act(stage, pl.ds(0, here), number, "wait_send")
        for k in range(here):
            for part in range(2):
                share(stage, k, part).wait_send()
    label_all().wait_send()
    for k in range(here):
        swap_all(0, k).wait_send()
    place_done.wait()
    heat_done.wait()
    for k in range(here):
        stay(k).wait()
        swap_all(1, k).wait_recv()
    for k in range(here):
        swap_all(1, k).wait_send()


def finish_kernel(heat_in, returned, place_in, heat_out, slopes_out):
    heat_out[...] = heat_in[...]
    for k in range(place_in.shape[0]):
        head, rest = two_halves(flat(returned[k]))
        place = place_in[k]
        slopes_out[k] = dot(
            jnp.concatenate([place, place], axis=1), jnp.concatenate([head, rest], axis=0)
        )


def finish(heat, returned, place):
    here, peers, capacity, cells = returned.shape
    blocks, slots = place.shape[1:]
    outs = (heat.shape, (here, blocks, cells))

    def spec(shape):
        return pl.BlockSpec((1, *shape[1:]), lambda k: (k,) + (0,) * (len(shape) - 1))

    return pl.pallas_call(
        finish_kernel,
        grid=(here,),
        out_shape=tuple(jax.ShapeDtypeStruct(x, jnp.float32) for x in outs),
        in_specs=[spec(heat.shape), spec(returned.shape), spec(place.shape)],
        out_specs=tuple(spec(x) for x in outs),
    )(heat, returned, place)


def local(parcel_patch, target_unit, target_patch, across_taps, down_taps, source_heated_mixing):
    here, blocks, cells = parcel_patch.shape
    terms, dies, _ = source_heated_mixing.shape
    peers = lax.axis_size(("row", "col"))
    capacity = max(2, 2 * blocks // peers)
    slots = peers * capacity
    a, b, h = UNIT_MESH_X, UNIT_MESH_Y, HALO
    w0, w1 = a + 2 * h, b + 2 * h
    anywhere = pl.BlockSpec(memory_space=pl.ANY)
    f32, bf16 = jnp.float32, jnp.bfloat16
    swap_buffer = pltpu.VMEM((here, peers, capacity, cells), f32)
    sems = pltpu.SemaphoreType.DMA
    heat, returned, place = pl.pallas_call(
        kernel,
        out_shape=(
            jax.ShapeDtypeStruct((here, a, b), f32),
            jax.ShapeDtypeStruct((here, peers, capacity, cells), f32),
            jax.ShapeDtypeStruct((here, blocks, slots), bf16),
        ),
        in_specs=[anywhere] * 5 + [pl.BlockSpec(memory_space=pltpu.SMEM)],
        out_specs=(anywhere,) * 3,
        scratch_shapes=[
            pltpu.VMEM(parcel_patch.shape, f32),
            pltpu.VMEM((here, blocks), jnp.int32),
            pltpu.VMEM((here, blocks), jnp.int32),
            pltpu.VMEM(across_taps.shape, f32),
            pltpu.VMEM(down_taps.shape, f32),
            pltpu.VMEM((here, a, b), f32),
            sems((5,)), sems((here + 2,)),
            swap_buffer, swap_buffer, swap_buffer,
            pltpu.VMEM((peers, 1, 128), f32),
            pltpu.VMEM((peers, 1, 128), f32),
            pltpu.VMEM((peers, 128), f32),
            pltpu.VMEM((here, blocks, slots), bf16),
            pltpu.VMEM((here, slots, (a // PATCH_SIDE) * (b // PATCH_SIDE)), bf16),
            pltpu.VMEM((2, here, w0, w1), f32),
            pltpu.VMEM((2, terms * a, 3 * a), bf16),
            pltpu.VMEM((2, terms * a, 6 * h), bf16),
            pltpu.VMEM((2, terms, 2 * w1, b), bf16),
            pltpu.VMEM((here, 3 * a, w1), bf16),
            pltpu.VMEM((here, 6 * h, w1), bf16),
            pltpu.VMEM((here, terms * a, w1), f32),
            pltpu.VMEM((here, terms * a, 2 * w1), bf16),
            pltpu.VMEM((here, terms, a, b), f32),
            pltpu.VMEM((2, dies, a, b), f32),
            pltpu.VMEM((2, here, a, b), f32),
            sems((2, here)), sems((2, here)), sems((2,)),
            sems((2, 8)), sems((2, here, 8)),
            sems((2, here, 2)), sems((2, here, 2)),
        ],
        compiler_params=pltpu.CompilerParams(
            collective_id=0, has_side_effects=True, vmem_limit_bytes=56 * 2**20
        ),
    )(
        parcel_patch, target_unit.reshape(here, blocks), target_patch,
        across_taps, down_taps, source_heated_mixing.transpose(1, 2, 0),
    )
    return finish(heat, returned, place)


def solution(mesh):
    placed = (
        P("die", ("row", "col"), None),
        P("die", ("row", "col"), None),
        P("die", ("row", "col")),
        P(),
        P(),
        P(),
    )
    return jax.shard_map(
        local,
        mesh=mesh,
        in_specs=placed,
        out_specs=(P("die", "row", "col"), P("die", ("row", "col"), None)),
        check_vma=False,
    )
```

```python
import functools

import jax
import jax.numpy as jnp
from jax import lax
from jax.experimental import pallas as pl
from jax.experimental.pallas import tpu as pltpu
from jax.sharding import PartitionSpec as P

PATCH_SIDE = 16
UNIT_MESH_X = 128
UNIT_MESH_Y = 256
HALO = 128
MESH = pl.DeviceIdType.MESH


def two_halves(values):
    head = values.astype(jnp.bfloat16)
    return head, (values - head.astype(jnp.float32)).astype(jnp.bfloat16)


def dot(left, right):
    return jnp.dot(left, right, preferred_element_type=jnp.float32)


def iota(shape, dim):
    return lax.broadcasted_iota(jnp.int32, shape, dim)


def exchange_blocks(x):
    rows = x.shape[0]
    left = x[:, :128].reshape(rows // 16, 2, 8, 128)
    right = x[:, 128:].reshape(rows // 16, 2, 8, 128)
    parts = [[left[:, 0], right[:, 0]], [left[:, 1], right[:, 1]]]
    parts[0][1], parts[1][0] = parts[1][0], parts[0][1]
    line, lane = iota((1, 8, 128), 1), iota((1, 8, 128), 2)

    def inner(v):
        for bit in range(3):
            d, w = 1 << bit, 16 << bit
            low_line, low_lane = (line & d) == 0, (lane & w) == 0
            first = pltpu.roll(pltpu.roll(v, 8 - d, 1), w, 2)
            second = first if bit == 2 else pltpu.roll(pltpu.roll(v, d, 1), 128 - w, 2)
            v = jnp.where(low_line == low_lane, v, jnp.where(low_line, first, second))
        return v

    columns = [
        jnp.stack([inner(parts[0][c]), inner(parts[1][c])], axis=1).reshape(rows, 128)
        for c in range(2)
    ]
    return jnp.concatenate(columns, axis=1)


def flat(parts):
    peers, capacity, cells = parts.shape
    if capacity % 8 == 0:
        return parts.reshape(peers * capacity, cells)
    return jnp.concatenate([parts[p] for p in range(peers)], axis=0)


def kernel(
    patch_in, unit_in, tile_in, across_in, down_in, mix_ref, heat_out, returned, place_out,
    patch_ref, unit_ref, tile_ref, across_ref, down_ref, heat_ref, in_sems, out_sems,
    outgoing, arrived, answers, label_out, label_in, label_rows,
    place_keep, chosen_keep, pads, a_own, a_halo, d_cat, p_own, p_halo, y_own, x_cat,
    z_all, acc, got, swap_send, swap_recv, label_sems, halo_send, halo_recv, die_send, die_recv,
):
    here, blocks, cells = patch_ref.shape
    terms = across_ref.shape[0]
    peers, capacity = outgoing.shape[1], outgoing.shape[2]
    slots = peers * capacity
    a, b, h = UNIT_MESH_X, UNIT_MESH_Y, HALO
    tiles = (a // PATCH_SIDE) * (b // PATCH_SIDE)
    row, col, die = lax.axis_index("row"), lax.axis_index("col"), lax.axis_index("die")
    rows_mesh, cols_mesh = lax.axis_size("row"), lax.axis_size("col")
    me = row * cols_mesh + col
    has_up, has_down = row > 0, row < rows_mesh - 1
    has_left, has_right = col > 0, col < cols_mesh - 1
    up, down, left, right = {"row": row - 1}, {"row": row + 1}, {"col": col - 1}, {"col": col + 1}
    other = {"die": 1 - die}

    def place_of(number):
        return {"row": number // cols_mesh, "col": number % cols_mesh}

    loads = [
        pltpu.make_async_copy(src, dst, in_sems.at[i])
        for i, (src, dst) in enumerate((
            (unit_in, unit_ref), (tile_in, tile_ref), (patch_in, patch_ref),
            (across_in, across_ref), (down_in, down_ref),
        ))
    ]
    for load in loads:
        load.start()
    barrier = pltpu.get_barrier_semaphore()

    def greet(i, carry):
        pl.semaphore_signal(barrier, inc=1, device_id=place_of((me + i) % peers), device_id_type=MESH)
        return carry

    lax.fori_loop(1, peers, greet, 0)
    pl.semaphore_signal(barrier, inc=1, device_id=other, device_id_type=MESH)

    for load in loads[:3]:
        load.wait()
    eye = iota((blocks, blocks), 0) == iota((blocks, blocks), 1)
    before = (iota((blocks, blocks), 1) < iota((blocks, blocks), 0)).astype(jnp.bfloat16)
    lanes = iota((blocks, 128), 1).astype(jnp.float32)
    slot_lane = iota((blocks, slots), 1).astype(jnp.float32)
    slot_line = iota((slots, blocks), 0).astype(jnp.float32)
    peer_line = iota((peers, blocks), 0).astype(jnp.float32)

    def column(line):
        return jnp.sum(jnp.where(eye, line, 0.0), axis=1, keepdims=True)

    def route(k):
        dest_row = unit_ref[k : k + 1, :].astype(jnp.float32)
        dest = column(dest_row)
        named = (dest == lanes).astype(jnp.bfloat16)
        count = dot(before, named)
        position = jnp.sum(named.astype(jnp.float32) * count, axis=1, keepdims=True)
        slot = dest * capacity + position
        slot_row = jnp.sum(jnp.where(eye, slot, 0.0), axis=0, keepdims=True)
        place_t = (slot_line == slot_row).astype(jnp.bfloat16)
        head, rest = two_halves(patch_ref[k])
        out = dot(
            jnp.concatenate([place_t, place_t], axis=1), jnp.concatenate([head, rest], axis=0)
        )
        for p in range(peers):
            outgoing[k, p] = out[p * capacity : (p + 1) * capacity]
        return dest_row, position, slot

    def label_part(k, dest_row, position):
        tile = column((tile_ref[k : k + 1, :] + 1).astype(jnp.float32))
        spread = jnp.where(lanes == position + k * capacity, tile, 0.0).astype(jnp.bfloat16)
        return dot((peer_line == dest_row).astype(jnp.bfloat16), spread)

    def swap_copy(stage, k, i):
        to = (me + i) % peers
        src, dst = (outgoing, arrived) if stage == 0 else (answers, returned)
        return pltpu.make_async_remote_copy(
            src_ref=src.at[k, to], dst_ref=dst.at[k, me],
            send_sem=swap_send.at[stage, k], recv_sem=swap_recv.at[stage, k],
            device_id=place_of(to), device_id_type=MESH,
        )

    def swap_all(stage, k):
        src, dst = (outgoing, arrived) if stage == 0 else (answers, returned)
        return pltpu.make_async_remote_copy(
            src_ref=src.at[k, pl.ds(0, peers - 1)], dst_ref=dst.at[k, pl.ds(0, peers - 1)],
            send_sem=swap_send.at[stage, k], recv_sem=swap_recv.at[stage, k],
            device_id=other, device_id_type=MESH,
        )

    def label_copy(i):
        to = (me + i) % peers
        return pltpu.make_async_remote_copy(
            src_ref=label_out.at[to], dst_ref=label_in.at[me],
            send_sem=label_sems.at[0], recv_sem=label_sems.at[1],
            device_id=place_of(to), device_id_type=MESH,
        )

    def label_all():
        return pltpu.make_async_remote_copy(
            src_ref=label_out.at[pl.ds(0, peers - 1)], dst_ref=label_in.at[pl.ds(0, peers - 1)],
            send_sem=label_sems.at[0], recv_sem=label_sems.at[1],
            device_id=other, device_id_type=MESH,
        )

    def start_each(make):
        def body(j, carry):
            make(j).start()
            return carry

        lax.fori_loop(1, peers, body, 0)

    routes = [route(0)]
    pl.semaphore_wait(barrier, peers)
    start_each(functools.partial(swap_copy, 0, 0))
    routes += [route(k) for k in range(1, here)]
    label_sum = sum(label_part(k, *routes[k][:2]) for k in range(here))
    for p in range(peers):
        label_out[p] = label_sum[p : p + 1]
    start_each(label_copy)
    for k in range(1, here):
        start_each(functools.partial(swap_copy, 0, k))
    label_in[me] = label_out[me]
    for k in range(here):
        place_keep[k] = (routes[k][2] == slot_lane).astype(jnp.bfloat16)
        arrived[k, me] = outgoing[k, me]
    place_done = pltpu.make_async_copy(place_keep, place_out, out_sems.at[0])
    place_done.start()

    w0, w1 = a + 2 * h, b + 2 * h
    for there, lines, cols in (
        (has_up, slice(0, h), slice(0, w1)),
        (has_down, slice(h + a, w0), slice(0, w1)),
        (has_left, slice(0, w0), slice(0, h)),
        (has_right, slice(0, w0), slice(h + b, w1)),
    ):
        @pl.when(jnp.logical_not(there))
        def _(lines=lines, cols=cols):
            part = pads[:, :, lines, cols]
            pads[:, :, lines, cols] = jnp.zeros_like(part)

    for load in loads[3:]:
        load.wait()
    u0, u1 = iota((across_ref.shape[1], 3 * h), 0), iota((across_ref.shape[1], 3 * h), 1)
    taps = across_ref.shape[1]

    def base(taps_ref, flipped):
        pick = (u1 == (taps - u0 if flipped else u0 + 1)).astype(jnp.float32)
        return jnp.dot(
            taps_ref[...], pick, precision=lax.Precision.HIGHEST, preferred_element_type=jnp.float32
        )

    none = jnp.zeros((h, h), jnp.bfloat16)
    for stage in range(2):
        across_base = base(across_ref, stage == 1)
        down_base = base(down_ref, stage == 0)
        for t in range(terms):
            lines = pl.ds(t * a, a)
            span = jnp.broadcast_to(across_base[t : t + 1, :], (a, 3 * h))
            head, rest = two_halves(pltpu.roll(span, 0, 1, stride=1, stride_axis=0))
            for part, piece in enumerate((head, head, rest)):
                a_own[stage, lines, part * a : (part + 1) * a] = piece[:, h : 2 * h]
                a_halo[stage, lines, part * 2 * h : part * 2 * h + h] = piece[:, :h]
                a_halo[stage, lines, part * 2 * h + h : (part + 1) * 2 * h] = piece[:, 2 * h :]
            wide = jnp.broadcast_to(down_base[t : t + 1, :], (3 * h, 3 * h))
            wide = pltpu.roll(wide, h, 1, stride=1, stride_axis=0)[:, :h]
            w = b + 2 * h
            for part, piece in enumerate(two_halves(wide)):
                at = part * w
                d_cat[stage, t, at : at + b, 0:h] = piece[h : 3 * h]
                d_cat[stage, t, at : at + b, h:b] = piece[0:b]
                d_cat[stage, t, at + b : at + b + h, 0:h] = piece[0:h]
                d_cat[stage, t, at + b : at + b + h, h:b] = none
                d_cat[stage, t, at + b + h : at + w, 0:h] = none
                d_cat[stage, t, at + b + h : at + w, h:b] = piece[2 * h :]

    tops, sizes, half = (0, h, h + a), (h, a, h), a // 2

    def halo(stage, which, number, part=None):
        def block(band, start, width):
            lines = pl.ds(tops[band], sizes[band]) if part is None else pl.ds(tops[band] + part * half, half)
            return pads.at[stage, which, lines, pl.ds(start, width)]

        if number == 0:
            src, dst, device = block(1, h, b), block(2, h, b), up
        elif number == 1:
            src, dst, device = block(1, h, b), block(0, h, b), down
        elif number < 5:
            src, dst, device = block(number - 2, h, h), block(number - 2, h + b, h), left
        else:
            src, dst, device = block(number - 5, b, h), block(number - 5, 0, h), right
        arrival = halo_recv.at[stage, which if isinstance(which, int) else 0, number]
        return pltpu.make_async_remote_copy(
            src_ref=src, dst_ref=dst, send_sem=halo_send.at[stage, number], recv_sem=arrival,
            device_id=device, device_id_type=MESH,
        )

    rows_of = (has_up, None, has_down)

    def both(x, y):
        return y if x is None else jnp.logical_and(x, y)

    sends = [has_up, has_down] + [both(r, has_left) for r in rows_of] + [both(r, has_right) for r in rows_of]
    gets = [has_down, has_up] + [both(r, has_right) for r in rows_of] + [both(r, has_left) for r in rows_of]

    def act(stage, which, number, what, part=None):
        @pl.when(gets[number] if what == "wait_recv" else sends[number])
        def _():
            getattr(halo(stage, which, number, part), what)()

    def begin_halo(stage, k, field, part):
        pads[stage, k, h + part * half : h + (part + 1) * half, h : h + b] = field
        if stage == 1 or part == 1:
            for number in (0, 1):
                act(stage, k, number, "start", part if stage == 1 else None)
        if part == 1:
            for number in (3, 6):
                act(stage, k, number, "start")

    def forward(stage, k):
        for from_down, corners in ((0, (4, 7)), (1, (2, 5))):
            act(stage, k, from_down, "wait_recv")
            for number in corners:
                act(stage, k, number, "start")

    def fill(stage, k, band, source, at, width):
        head, rest = two_halves(pads[stage, k, tops[band] : tops[band] + sizes[band], source : source + width])
        cols = slice(at, at + width)
        if band == 1:
            for part, piece in enumerate((head, rest, head)):
                p_own[k, part * a : (part + 1) * a, cols] = piece
        else:
            off = 0 if band == 0 else h
            for part, piece in enumerate((head, rest, head)):
                p_halo[k, part * 2 * h + off : part * 2 * h + off + h, cols] = piece

    def own_rows(stage, k, at):
        cols = slice(at, at + b)
        y_own[k, :, cols] = dot(a_own[stage], p_own[k, :, cols])

    def far_rows(stage, k, at):
        cols = slice(at, at + b)
        total = dot(a_halo[stage], p_halo[k, :, cols]) + y_own[k, :, cols]
        head, rest = two_halves(total)
        x_cat[k, :, cols] = head
        x_cat[k, :, at + b + 2 * h : at + 2 * b + 2 * h] = rest

    def along(stage, k, at):
        w = b + 2 * h
        head_cols, rest_cols = slice(at, at + b), slice(w + at, w + at + b)

        def step(t, carry):
            lines = pl.ds(pl.multiple_of(t * a, a), a)
            head, rest = x_cat[k, lines, head_cols], x_cat[k, lines, rest_cols]
            d_head, d_rest = d_cat[stage, t, head_cols], d_cat[stage, t, rest_cols]
            z = dot(
                jnp.concatenate([head, head, rest], axis=1),
                jnp.concatenate([d_head, d_rest, d_head], axis=0),
            )
            z_all[k, t] = z if at == 0 else z_all[k, t] + z
            return carry

        lax.fori_loop(0, terms, step, 0, unroll=True)

    def mix(stage, d, part):
        target = ((1 - die) if d < here else die) * here + d % here
        weights = []
        for k in range(here):
            source = die * here + k
            for t in range(terms):
                pair = (target, source) if stage == 0 else (source, target)
                weights.append(mix_ref[pair[0], pair[1], t])

        def step(i, carry):
            lines = pl.ds(pl.multiple_of(part * half + i * 16, 16), 16)
            total = jnp.zeros((16, b), jnp.float32)
            for k in range(here):
                for t in range(terms):
                    total = total + weights[k * terms + t] * z_all[k, t, lines]
            acc[stage, d, lines] = total
            return carry

        lax.fori_loop(0, half // 16, step, 0)

    def share(stage, k, part):
        lines = pl.ds(part * half, half)
        return pltpu.make_async_remote_copy(
            src_ref=acc.at[stage, k, lines], dst_ref=got.at[stage, k, lines],
            send_sem=die_send.at[stage, k, part], recv_sem=die_recv.at[stage, k, part],
            device_id=other, device_id_type=MESH,
        )

    def far_middle(stage, k):
        for band in (0, 2):
            fill(stage, k, band, h, 0, b)
        far_rows(stage, k, 0)

    def own_sides(stage, k):
        for number in (3, 6):
            act(stage, k, number, "wait_recv")
        fill(stage, k, 1, 0, b, h)
        fill(stage, k, 1, h + b, b + h, h)
        own_rows(stage, k, b)

    def far_sides(stage, k):
        for number in (2, 4, 5, 7):
            act(stage, k, number, "wait_recv")
        for band in (0, 2):
            fill(stage, k, band, 0, b, h)
            fill(stage, k, band, h + b, b + h, h)
        far_rows(stage, k, b)

    def run_stage(stage):
        own_sides(stage, 0)
        for k in range(here):
            if k == 0:
                forward(stage, k)
            far_middle(stage, k)
            along(stage, k, 0)
            far_sides(stage, k)
            if k + 1 < here:
                own_sides(stage, k + 1)
                forward(stage, k + 1)
            along(stage, k, b)
        for k in range(here):
            for part in range(2):
                mix(stage, k, part)
                share(stage, k, part).start()
        for k in range(here):
            for part in range(2):
                mix(stage, here + k, part)

    label_all().wait_recv()
    for p in range(peers):
        label_rows[p : p + 1] = label_in[p]
    label_flat = label_rows[...].astype(jnp.bfloat16)
    lane_of = iota((128, slots), 1) % capacity
    held = iota((peers, slots), 1) // capacity == iota((peers, slots), 0)
    tile_line = (iota((tiles, slots), 0) + 1).astype(jnp.float32)
    tile_lane = (iota((slots, tiles), 1) + 1).astype(jnp.float32)
    eye_slots = iota((slots, slots), 0) == iota((slots, slots), 1)
    for k in range(here):
        pick = (iota((128, slots), 0) == lane_of + k * capacity).astype(jnp.bfloat16)
        label = jnp.sum(jnp.where(held, dot(label_flat, pick), 0.0), axis=0, keepdims=True)
        chosen_t = (tile_line == label).astype(jnp.bfloat16)
        label_col = jnp.sum(jnp.where(eye_slots, label, 0.0), axis=1, keepdims=True)
        chosen_keep[k] = (tile_lane == label_col).astype(jnp.bfloat16)
        swap_all(0, k).wait_recv()
        head, rest = two_halves(flat(arrived[k]))
        totals = dot(
            jnp.concatenate([chosen_t, chosen_t], axis=1), jnp.concatenate([head, rest], axis=0)
        )
        field = exchange_blocks(totals)
        for part in range(2):
            begin_halo(0, k, field[part * half : (part + 1) * half], part)
        fill(0, k, 1, h, 0, b)
        own_rows(0, k, 0)
    run_stage(0)
    for k in range(here):
        for part in range(2):
            share(0, k, part).wait_recv()
            lines = slice(part * half, (part + 1) * half)
            heat = acc[0, here + k, lines] + got[0, k, lines]
            heat_ref[k, lines] = heat
            begin_halo(1, k, jax.nn.sigmoid(heat), part)
        fill(1, k, 1, h, 0, b)
        own_rows(1, k, 0)
    def stay(k):
        return pltpu.make_async_copy(answers.at[k, me], returned.at[k, me], out_sems.at[2 + k])

    heat_done = pltpu.make_async_copy(heat_ref, heat_out, out_sems.at[1])
    heat_done.start()
    run_stage(1)
    for k in range(here):
        for part in range(2):
            share(1, k, part).wait_recv()
        patches = exchange_blocks(acc[1, here + k] + got[1, k])
        head, rest = two_halves(patches)
        chosen = chosen_keep[k]
        answer = dot(jnp.concatenate([chosen, chosen], axis=1), jnp.concatenate([head, rest], axis=0))
        for p in range(peers):
            answers[k, p] = answer[p * capacity : (p + 1) * capacity]
        start_each(functools.partial(swap_copy, 1, k))
        stay(k).start()
    for stage in range(2):
        for number in range(8):
            act(stage, pl.ds(0, here), number, "wait_send")
        for k in range(here):
            for part in range(2):
                share(stage, k, part).wait_send()
    label_all().wait_send()
    for k in range(here):
        swap_all(0, k).wait_send()
    place_done.wait()
    heat_done.wait()
    for k in range(here):
        stay(k).wait()
        swap_all(1, k).wait_recv()
    for k in range(here):
        swap_all(1, k).wait_send()


def finish_kernel(heat_in, returned, place_in, heat_out, slopes_out):
    heat_out[...] = heat_in[...]
    for k in range(place_in.shape[0]):
        head, rest = two_halves(flat(returned[k]))
        place = place_in[k]
        slopes_out[k] = dot(
            jnp.concatenate([place, place], axis=1), jnp.concatenate([head, rest], axis=0)
        )


def finish(heat, returned, place):
    here, peers, capacity, cells = returned.shape
    blocks, slots = place.shape[1:]
    outs = (heat.shape, (here, blocks, cells))

    def spec(shape):
        return pl.BlockSpec((1, *shape[1:]), lambda k: (k,) + (0,) * (len(shape) - 1))

    return pl.pallas_call(
        finish_kernel,
        grid=(here,),
        out_shape=tuple(jax.ShapeDtypeStruct(x, jnp.float32) for x in outs),
        in_specs=[spec(heat.shape), spec(returned.shape), spec(place.shape)],
        out_specs=tuple(spec(x) for x in outs),
    )(heat, returned, place)


def local(parcel_patch, target_unit, target_patch, across_taps, down_taps, source_heated_mixing):
    here, blocks, cells = parcel_patch.shape
    terms, dies, _ = source_heated_mixing.shape
    peers = lax.axis_size(("row", "col"))
    capacity = max(2, 2 * blocks // peers)
    slots = peers * capacity
    a, b, h = UNIT_MESH_X, UNIT_MESH_Y, HALO
    w0, w1 = a + 2 * h, b + 2 * h
    anywhere = pl.BlockSpec(memory_space=pl.ANY)
    f32, bf16 = jnp.float32, jnp.bfloat16
    swap_buffer = pltpu.VMEM((here, peers, capacity, cells), f32)
    sems = pltpu.SemaphoreType.DMA
    heat, returned, place = pl.pallas_call(
        kernel,
        out_shape=(
            jax.ShapeDtypeStruct((here, a, b), f32),
            jax.ShapeDtypeStruct((here, peers, capacity, cells), f32),
            jax.ShapeDtypeStruct((here, blocks, slots), bf16),
        ),
        in_specs=[anywhere] * 5 + [pl.BlockSpec(memory_space=pltpu.SMEM)],
        out_specs=(anywhere,) * 3,
        scratch_shapes=[
            pltpu.VMEM(parcel_patch.shape, f32),
            pltpu.VMEM((here, blocks), jnp.int32),
            pltpu.VMEM((here, blocks), jnp.int32),
            pltpu.VMEM(across_taps.shape, f32),
            pltpu.VMEM(down_taps.shape, f32),
            pltpu.VMEM((here, a, b), f32),
            sems((5,)), sems((here + 2,)),
            swap_buffer, swap_buffer, swap_buffer,
            pltpu.VMEM((peers, 1, 128), f32),
            pltpu.VMEM((peers, 1, 128), f32),
            pltpu.VMEM((peers, 128), f32),
            pltpu.VMEM((here, blocks, slots), bf16),
            pltpu.VMEM((here, slots, (a // PATCH_SIDE) * (b // PATCH_SIDE)), bf16),
            pltpu.VMEM((2, here, w0, w1), f32),
            pltpu.VMEM((2, terms * a, 3 * a), bf16),
            pltpu.VMEM((2, terms * a, 6 * h), bf16),
            pltpu.VMEM((2, terms, 2 * w1, b), bf16),
            pltpu.VMEM((here, 3 * a, w1), bf16),
            pltpu.VMEM((here, 6 * h, w1), bf16),
            pltpu.VMEM((here, terms * a, w1), f32),
            pltpu.VMEM((here, terms * a, 2 * w1), bf16),
            pltpu.VMEM((here, terms, a, b), f32),
            pltpu.VMEM((2, dies, a, b), f32),
            pltpu.VMEM((2, here, a, b), f32),
            sems((2, here)), sems((2, here)), sems((2,)),
            sems((2, 8)), sems((2, here, 8)),
            sems((2, here, 2)), sems((2, here, 2)),
        ],
        compiler_params=pltpu.CompilerParams(
            collective_id=0, has_side_effects=True, vmem_limit_bytes=56 * 2**20
        ),
    )(
        parcel_patch, target_unit.reshape(here, blocks), target_patch,
        across_taps, down_taps, source_heated_mixing.transpose(1, 2, 0),
    )
    return finish(heat, returned, place)


def solution(mesh):
    placed = (
        P("die", ("row", "col"), None),
        P("die", ("row", "col"), None),
        P("die", ("row", "col")),
        P(),
        P(),
        P(),
    )
    return jax.shard_map(
        local,
        mesh=mesh,
        in_specs=placed,
        out_specs=(P("die", "row", "col"), P("die", ("row", "col"), None)),
        check_vma=False,
    )
```
